32 devices in a mesh: dp: 8 (over z, y), seq: 4 (over x, core).
Axes of the slice: x: 2, y: 2, z: 4, core: 2. Of those that a mesh axis runs over, the one named last changes fastest.
Arguments:
- inputs: float32 [8, 1024, 2048], P('dp', 'seq'), may hold values from -6 to 6
- segments: int32 [8, 1024], P('dp', 'seq'), may hold values from 0 to 31, as said below
- valid_count: int32 [8], P('dp'), may hold values from 512 to 1024
- teacher: float32 [8, 1024, 2048], P('dp', 'seq'), may hold values from -6 to 6
- cotangent: float32 [8, 1024, 2048], P('dp', 'seq'), may hold values from -6 to 6
- w_proj: bfloat16 [2048, 8192], P('dp'), may hold values from -0.125 to 0.125
- w_decay: bfloat16 [2048, 16], P('dp'), may hold values from -0.25 to 0.25
- b_decay: float32 [16], replicated, may hold values from 1 to 5
- w_out: bfloat16 [2048, 2048], P('dp'), may hold values from -0.125 to 0.125
- gain_ret: float32 [2048], replicated, may hold values from 0.5 to 1.5
- gain_ffn: float32 [2048], replicated, may hold values from 0.5 to 1.5
- w_gu: bfloat16 [2048, 11008], P('dp'), may hold values from -0.125 to 0.125
- w_down: bfloat16 [5504, 2048], P('dp'), may hold values from -0.078125 to 0.078125
Outputs:
- output: float32 [8, 1024, 2048], P('dp', 'seq')
- grad_inputs: float32 [8, 1024, 2048], P('dp', 'seq')
- grad_w_proj: float32 [2048, 8192], P('dp')
- grad_w_decay: float32 [2048, 16], P('dp')
- grad_b_decay: float32 [16], replicated
- grad_w_out: float32 [2048, 2048], P('dp')
- grad_gain_ret: float32 [2048], replicated
- grad_gain_ffn: float32 [2048], replicated
- grad_w_gu: float32 [2048, 11008], P('dp')
- grad_w_down: float32 [5504, 2048], P('dp')
- mse: float32 [], replicated
The draws below stay inside these ranges and needn't reach their ends.
Inputs may be any that keep to these rules, and one draw needn't show every extreme that they name: `segments`: within a row the numbers never fall and each number is one run of positions; different rows use different numbers.
All inputs are finite; a program needn't handle non-finite values.
Results may differ from the reference program's by a relative error of at most 0.018.
Values may be sent and summed in bfloat16 or wider, within the bound.
A program may use at most 448 MiB of HBM per device.

```python
import jax
import jax.numpy as jnp
from jax import lax

D = 2048
HEADS = 16
HEAD_DIM = 128
FF = 5504
TOK_DEV = 256
ROW = 1024
GROUPS = 8


def draw_segments(key, part):
    kind_key = jax.random.fold_in(key, 5)
    first_key = jax.random.fold_in(key, 11)
    last_key = jax.random.fold_in(key, 23)
    border_key = jax.random.fold_in(key, 31)
    device_key = jax.random.fold_in(key, 37)
    start_key = jax.random.fold_in(key, 41)
    width_key = jax.random.fold_in(key, 43)
    quarter = max(TOK_DEV // 4, 1)
    half_dev = max(TOK_DEV // 2, 2)
    seq_count = ROW // TOK_DEV
    offset = jax.random.randint(kind_key, (), 0, 2)
    kind_two = (jnp.arange(GROUPS, dtype=jnp.int32)[:, None] + offset) % 2 == 1
    position = jnp.arange(ROW, dtype=jnp.int32)[None, :]
    first_cut = jax.random.randint(first_key, (GROUPS, 1), 1, quarter + 1)
    last_cut = jax.random.randint(last_key, (GROUPS, 1), ROW - quarter, ROW)
    spanning = (position >= first_cut).astype(jnp.int32) + 2 * (position >= last_cut).astype(jnp.int32)
    border = TOK_DEV * jax.random.randint(border_key, (GROUPS, 1), 1, seq_count)
    middle = jax.random.randint(device_key, (GROUPS, 1), 1, max(seq_count - 1, 2))
    short_start = middle * TOK_DEV + jax.random.randint(start_key, (GROUPS, 1), 1, half_dev)
    short_end = short_start + jax.random.randint(width_key, (GROUPS, 1), 1, half_dev)
    broken = (position >= border).astype(jnp.int32) + (position >= short_start).astype(jnp.int32) + (position >= short_end).astype(jnp.int32)
    local_part = jnp.where(kind_two, broken, spanning)
    row_base = 4 * jnp.arange(GROUPS, dtype=jnp.int32)[:, None]
    return row_base + local_part


def touch_ends(values, stream_key, low, largest):
    extent = values.shape
    place = [jax.random.randint(jax.random.fold_in(stream_key, axis), (), 0, extent[axis]) for axis in range(len(extent))]
    values = values.at[tuple(place)].set(low)
    longest = extent.index(max(extent))
    place[longest] = (place[longest] + 1) % extent[longest]
    return values.at[tuple(place)].set(largest)


def level_of(own_key, dims, split, smallest, largest):
    loudness, own = 1.0, jax.random.fold_in(own_key, 6)
    for dim, blocks in split:
        draws = jnp.exp(jax.random.uniform(jax.random.fold_in(own, dim), (blocks,), jnp.float32, smallest / len(split), largest / len(split)))
        loudness = loudness * jnp.repeat(draws, dims[dim] // blocks).reshape([-1 if axis == dim else 1 for axis in range(len(dims))])
    return loudness


def bell_draw(stream_key, shape, width, bound, pieces=(), kind=jnp.bfloat16):
    values = jax.random.normal(stream_key, shape, jnp.float32) * width
    if len(pieces) > 0:
        values = level_of(stream_key, shape, pieces, -0.22, 0.18) * values
    return jnp.clip(values, min=-bound, max=bound).astype(kind)


def setup_inputs(seed: int = 0) -> dict:
    arg_keys = jax.random.split(jax.random.key(seed), 14)
    return {
        "inputs": bell_draw(arg_keys[0], (GROUPS, ROW, D), 1.0, 6.0, ((0, 8), (1, 4)), jnp.float32),
        "segments": draw_segments(jax.random.fold_in(arg_keys[13], 71), 0),
        "valid_count": touch_ends(jax.random.randint(arg_keys[2], (GROUPS,), ROW // 2, ROW + 1), jax.random.fold_in(arg_keys[2], 1), ROW // 2, ROW).astype(jnp.int32),
        "teacher": bell_draw(arg_keys[3], (GROUPS, ROW, D), 1.0, 6.0, ((0, 8), (1, 4)), jnp.float32),
        "cotangent": bell_draw(arg_keys[4], (GROUPS, ROW, D), 1.0, 6.0, ((0, 8), (1, 4)), jnp.float32),
        "w_proj": bell_draw(arg_keys[5], (D, 4 * D), D ** -0.5, 0.125, ((0, 8),)),
        "w_decay": bell_draw(arg_keys[6], (D, HEADS), (D // 4) ** -0.5, 0.25, ((0, 8),)),
        "b_decay": jnp.clip(jax.random.uniform(arg_keys[7], (HEADS,), jnp.float32, 1.0, 5.0), 1.0, 5.0),
        "w_out": bell_draw(arg_keys[8], (D, D), D ** -0.5, 0.125, ((0, 8),)),
        "gain_ret": jnp.clip(1.0 + 0.1 * jax.random.normal(arg_keys[9], (D,), jnp.float32), 0.5, 1.5),
        "gain_ffn": jnp.clip(1.0 + 0.1 * jax.random.normal(arg_keys[10], (D,), jnp.float32), 0.5, 1.5),
        "w_gu": bell_draw(arg_keys[11], (D, 2 * FF), D ** -0.5, 0.125, ((0, 8),)),
        "w_down": bell_draw(arg_keys[12], (FF, D), FF ** -0.5, 0.078125, ((0, 8),)),
    }


@jax.custom_vjp
def low(v):
    return lax.optimization_barrier(v.astype(jnp.bfloat16)).astype(jnp.float32)

@jax.custom_vjp
def low_back(v):
    return v

def low_keep(v):
    return (low(v), None)

def low_pass(kept, grad):
    return (grad,)

def back_keep(v):
    return (v, None)

def back_low(kept, grad):
    return (low(grad),)
low.defvjp(low_keep, low_pass)
low_back.defvjp(back_keep, back_low)

def matmul_high(left, right):
    return jnp.dot(left, right, precision=lax.Precision.HIGHEST, preferred_element_type=jnp.float32)

def split_heads(matrix):
    return matrix.reshape(matrix.shape[0], HEADS, HEAD_DIM).transpose(1, 0, 2)

def one_head(query_head, key_head, value_head, cumulative, allowed):
    spread = cumulative[:, None] - cumulative[None, :]
    decay = jnp.where(allowed, jnp.exp(jnp.where(allowed, spread, jnp.zeros_like(spread))), jnp.zeros_like(spread))
    scores = matmul_high(query_head, key_head.T) * decay
    return matmul_high(scores, value_head)

def finish(merged, outgate):
    count = merged.shape[0]
    per_head = merged.reshape(count, HEADS, HEAD_DIM)
    normal = per_head * lax.rsqrt(jnp.maximum(lax.optimization_barrier(jnp.mean(per_head * per_head, axis=2, keepdims=True)), 1.0))
    return jax.nn.silu(outgate) * normal.reshape(count, D)

def layer_row(tokens, row_segments, proj_w, decay_w, bias_decay, out_w, gain_one, gain_two, gu_w, down_w):
    count = tokens.shape[0]
    scale_one = lax.rsqrt(lax.optimization_barrier(jnp.mean(tokens * tokens, axis=1, keepdims=True)) + 1e-06)
    normed = low(tokens * scale_one * gain_one)
    projected = low_back(matmul_high(normed, proj_w))
    queries = low(projected[:, :D] * HEAD_DIM ** (-0.5))
    key_rows = low(projected[:, D:2 * D])
    values = low(projected[:, 2 * D:3 * D])
    outgate = projected[:, 3 * D:]
    logdecay = jax.nn.log_sigmoid(low_back(matmul_high(normed, decay_w)) + bias_decay) / 16.0
    cumulative = jnp.cumsum(logdecay, axis=0)
    order = jnp.arange(count, dtype=jnp.int32)
    allowed = (row_segments[:, None] == row_segments[None, :]) & (order[:, None] >= order[None, :])

    def head_step(bundle):
        return one_head(bundle[0], bundle[1], bundle[2], bundle[3], allowed)
    retained = lax.map(jax.checkpoint(head_step), (split_heads(queries), split_heads(key_rows), split_heads(values), cumulative.T))
    merged = retained.transpose(1, 0, 2).reshape(count, D)
    gated_out = low(finish(merged, outgate))
    mixed = tokens + low_back(matmul_high(gated_out, out_w))
    scale_two = lax.rsqrt(lax.optimization_barrier(jnp.mean(mixed * mixed, axis=1, keepdims=True)) + 1e-06)
    normed_ffn = low(mixed * scale_two * gain_two)
    gate_up = low_back(matmul_high(normed_ffn, gu_w))
    activated = low(jax.nn.silu(gate_up[:, :FF]) * gate_up[:, FF:])
    return mixed + low_back(matmul_high(activated, down_w))

def reference(inputs, segments, valid_count, teacher, cotangent, w_proj, w_decay, b_decay, w_out, gain_ret, gain_ffn, w_gu, w_down):

    def forward_all(tokens, proj_w, decay_w, bias_decay, out_w, gain_one, gain_two, gu_w, down_w):

        def one_row(bundle):
            return layer_row(bundle[0], bundle[1], proj_w, decay_w, bias_decay, out_w, gain_one, gain_two, gu_w, down_w)
        return lax.map(jax.checkpoint(one_row), (tokens, segments))
    output, pullback = jax.vjp(forward_all, inputs, w_proj.astype(jnp.float32), w_decay.astype(jnp.float32), b_decay, w_out.astype(jnp.float32), gain_ret, gain_ffn, w_gu.astype(jnp.float32), w_down.astype(jnp.float32))
    valid_mask = (jnp.arange(ROW, dtype=jnp.int32)[None, :] < valid_count[:, None]).astype(jnp.float32)[:, :, None]
    mismatch = output - teacher
    grad_out = cotangent + valid_mask * mismatch
    grads = pullback(grad_out)
    total_valid = jnp.sum(valid_count).astype(jnp.float32)
    mse = jnp.sum(valid_mask * mismatch * mismatch) / (total_valid * D)
    return (output, grads[0], grads[1], grads[2], grads[3], grads[4], grads[5], grads[6], grads[7], grads[8], mse)
```

```python
import jax
import jax.numpy as jnp
from jax import lax
from jax.sharding import PartitionSpec as P

LOW = jnp.bfloat16
WIDE = jnp.float32


def dot(left, right, left_dim=1, right_dim=0):
    return lax.dot_general(
        left, right, (((left_dim,), (right_dim,)), ((), ())), preferred_element_type=WIDE
    )


def batch_dot(left, right, left_dim, right_dim):
    return lax.dot_general(
        left, right, (((left_dim,), (right_dim,)), ((0,), (0,))), preferred_element_type=WIDE
    )


def blocks_at(matrix, places, size, axis):
    return jnp.concatenate(
        [lax.dynamic_slice_in_dim(matrix, place * size, size, axis) for place in places], axis=axis
    )


def pick(index, choices):
    chosen = choices[-1]
    for number in range(len(choices) - 2, -1, -1):
        chosen = jnp.where(index == number, choices[number], chosen)
    return chosen


class Links:
    def __init__(self, dp_count, seq_count):
        self.dp_count, self.seq_count = dp_count, seq_count
        self.ring = dp_count // 2
        self.me_dp, self.me_seq = lax.axis_index("dp"), lax.axis_index("seq")
        self.turn, self.side = self.me_dp // 2, self.me_dp % 2
        self.past = {}

    def send(self, value, axis, pairs, stream=None, depth=2):
        if stream is not None:
            past = self.past.setdefault(stream, [])
            if len(past) >= depth:
                value, unused = lax.optimization_barrier((value, past[-depth]))
        moved = lax.ppermute(value, axis, pairs)
        if stream is not None:
            past.append(moved)
        return moved

    def around(self, value, stream=None):
        pairs = [(d, (d + 2) % self.dp_count) for d in range(self.dp_count)]
        return self.send(value, "dp", pairs, stream)

    def across(self, value, stream=None):
        return self.send(value, "dp", [(d, d ^ 1) for d in range(self.dp_count)], stream)

    def core(self, value):
        return self.send(value, "seq", [(s, s ^ 1) for s in range(self.seq_count)])

    def chip(self, value):
        return self.send(value, "seq", [(s, s ^ 2) for s in range(self.seq_count)])

    def sources(self):
        return [
            ((self.turn - r) % self.ring) * 2 + (self.side ^ e)
            for r in range(self.ring)
            for e in range(2)
        ]

    def places(self):
        return [
            ((self.turn - d // 2) % self.ring) * 2 + (self.side ^ (d % 2))
            for d in range(self.dp_count)
        ]

    def gather(self, block, streams=("ring", "pair")):
        own = [block]
        for unused in range(self.ring - 1):
            own.append(self.around(own[-1], streams[0]))
        other = [self.across(piece, streams[1]) for piece in own]
        return [piece for both in zip(own, other) for piece in both]

    def gather_pairs(self, block, streams=("ring", "pair")):
        pieces = [jnp.stack([block, self.across(block, streams[1])])]
        for unused in range(self.ring - 1):
            pieces.append(self.around(pieces[-1], streams[0]))
        return pieces

    def ring_sum(self, parts, stream="ring"):
        running = parts[1].astype(LOW)
        for r in range(2, self.ring):
            running = (self.around(running, stream).astype(WIDE) + parts[r].astype(WIDE)).astype(LOW)
        return self.around(running, stream).astype(WIDE) + parts[0].astype(WIDE)

    def scatter(self, own, other, streams=("ring", "pair")):
        sums = []
        for r in list(range(1, self.ring)) + [0]:
            come = self.across(other[r], streams[1])
            sums.append((own[r].astype(WIDE) + come.astype(WIDE)).astype(LOW))
        sums = sums[-1:] + sums[:-1]
        return self.ring_sum(sums, streams[0]).astype(LOW)

    def tokens_in(self, value):
        far = self.chip(value)
        near = self.core(value)
        return [value, near, far, self.core(far)]

    def tokens_out(self, parts):
        come_far = self.core(parts[3].astype(LOW))
        come_own = self.core(parts[1].astype(LOW))
        far = (parts[2] + come_far.astype(WIDE)).astype(LOW)
        return parts[0] + come_own.astype(WIDE) + self.chip(far).astype(WIDE)

    def in_order(self, pieces):
        return [
            pick(self.me_seq, [pieces[k ^ s] for s in range(self.seq_count)])
            for k in range(self.seq_count)
        ]


class Placed:
    def __init__(self, links, heads, hidden):
        self.links = links
        self.heads, self.width = heads, heads // links.seq_count
        shard = hidden // links.dp_count
        self.shard = shard
        self.part = -(-shard // (16 * links.seq_count)) * 16
        self.units = self.part * links.dp_count

    def to_rel(self, value):
        links = self.links
        return blocks_at(value, links.sources(), value.shape[1] // links.dp_count, 1)

    def from_rel(self, value):
        links = self.links
        return blocks_at(value, links.places(), value.shape[1] // links.dp_count, 1)

    def proj(self, weight):
        size = weight.shape[1] // (4 * self.heads)
        columns = [(b * self.width + j) * self.links.seq_count for b in range(4) for j in range(self.width)]
        block = blocks_at(weight, [at + self.links.me_seq for at in columns], size, 1)
        return jnp.concatenate(self.links.gather(block), axis=0)

    def decay(self, weight):
        pieces = self.links.gather_pairs(weight, (None, None))
        return jnp.concatenate([piece.reshape(-1, weight.shape[1]) for piece in pieces], axis=0)

    def out(self, weight):
        links = self.links
        size = weight.shape[0] // 2
        own = lax.dynamic_slice_in_dim(weight, (links.me_seq % 2) * size, size, 0)
        block = jnp.where(links.side == links.me_seq // 2, own, links.across(own, "pair"))
        pieces = [block]
        for unused in range(links.ring - 1):
            pieces.append(links.around(pieces[-1], "ring"))
        stacked = jnp.concatenate(pieces, axis=0)
        return blocks_at(stacked, [(links.turn - j) % links.ring for j in range(links.ring)], size, 0)

    def gate_up(self, weight):
        links = self.links
        pieces = []
        for start in range(0, weight.shape[1], self.shard):
            piece = weight[:, start : start + self.shard]
            piece = jnp.pad(piece, ((0, 0), (0, self.part * links.seq_count - self.shard)))
            pieces.append(
                lax.dynamic_slice_in_dim(piece, links.me_seq * self.part, self.part, 1)
            )
        half = len(pieces) // 2
        gate, up = (jnp.concatenate(pieces[:half], axis=1), jnp.concatenate(pieces[half:], axis=1))
        block = jnp.concatenate([gate, up], axis=1)
        return jnp.concatenate(links.gather(block), axis=0)

    def down(self, weight):
        links = self.links
        padded = jnp.pad(weight, ((0, self.part * links.seq_count - self.shard), (0, 0)))
        block = lax.dynamic_slice_in_dim(padded, links.me_seq * self.part, self.part, 0)
        stacked = jnp.concatenate(links.gather(block), axis=0)
        return blocks_at(stacked, links.places(), self.part, 0)

    def grad_down(self, grad):
        links = self.links
        blocks = [
            lax.dynamic_slice_in_dim(grad, place * self.part, self.part, 0) for place in links.sources()
        ]
        total = links.scatter(blocks[0::2], blocks[1::2])
        pieces = links.in_order(links.tokens_in(total))
        return jnp.concatenate(pieces, axis=0)[: self.shard].astype(WIDE)

    def split_rel(self, grad):
        size = grad.shape[0] // self.links.dp_count
        blocks = [grad[i * size : (i + 1) * size] for i in range(self.links.dp_count)]
        return blocks[0::2], blocks[1::2]

    def grad_gate_up(self, grad):
        links = self.links
        total = links.scatter(*self.split_rel(grad))
        pieces = links.in_order(links.tokens_in(total))
        rows = []
        for block in range(2 * links.dp_count):
            whole = jnp.concatenate(
                [piece[:, block * self.part : (block + 1) * self.part] for piece in pieces], axis=1
            )
            rows.append(whole[:, : self.shard])
        return jnp.concatenate(rows, axis=1).astype(WIDE)

    def grad_proj(self, grad):
        links = self.links
        total = links.scatter(*self.split_rel(grad))
        pieces = links.in_order(links.tokens_in(total))
        size = total.shape[1] // (4 * self.width)
        columns = [
            piece[:, at * size : (at + 1) * size] for at in range(4 * self.width) for piece in pieces
        ]
        return jnp.concatenate(columns, axis=1).astype(WIDE)

    def grad_decay(self, grad):
        links = self.links
        own, other = self.split_rel(grad)
        come = links.across(jnp.stack(other).astype(LOW))
        sums = (jnp.stack(own) + come.astype(WIDE)).astype(LOW)
        total = links.ring_sum([sums[r] for r in range(links.ring)], None).astype(LOW)
        pieces = links.in_order(links.tokens_in(total))
        return jnp.stack(pieces, axis=2).reshape(total.shape[0], -1).astype(WIDE)

    def grad_out(self, grad):
        links = self.links
        size = grad.shape[0] // links.ring
        parts = [
            lax.dynamic_slice_in_dim(grad, ((links.turn - r) % links.ring) * size, size, 0)
            for r in range(links.ring)
        ]
        total = links.ring_sum(parts, "ring").astype(LOW)
        come = links.across(total, "pair")
        mine = (total.astype(WIDE) + come.astype(WIDE)).astype(LOW)
        near = links.core(mine)
        first = links.me_seq % 2 == 0
        pair = jnp.concatenate([jnp.where(first, mine, near), jnp.where(first, near, mine)], axis=0)
        far = links.chip(pair)
        return jnp.where(links.me_seq // 2 == links.side, pair, far).astype(WIDE)

    def head_columns(self, table):
        return jnp.concatenate(
            [
                lax.dynamic_slice_in_dim(table, j * self.links.seq_count + self.links.me_seq, 1, table.ndim - 1)
                for j in range(self.width)
            ],
            axis=table.ndim - 1,
        )


class Plain:
    def __init__(self, dp_count, seq_count, heads, hidden):
        self.dp_count, self.seq_count = dp_count, seq_count
        self.me_seq = lax.axis_index("seq")
        self.heads, self.width = heads, heads // seq_count
        self.units = hidden // seq_count

    def to_rel(self, value):
        return value

    def from_rel(self, value):
        return value

    def mine(self, value, axis):
        return lax.dynamic_index_in_dim(value, self.me_seq, axis, keepdims=False)

    def spread(self, value, axis):
        wide = jnp.expand_dims(value, axis)
        wide = jnp.concatenate(
            [jnp.where(self.me_seq == s, wide, jnp.zeros_like(wide)) for s in range(self.seq_count)], axis
        )
        return wide

    def proj(self, weight):
        rows = weight.shape[0]
        block = self.mine(weight.reshape(rows, 4 * self.width, self.seq_count, -1), 2).reshape(rows, -1)
        return lax.all_gather(block, "dp", axis=0, tiled=True)

    def decay(self, weight):
        return lax.all_gather(weight, "dp", axis=0, tiled=True)

    def out(self, weight):
        whole = lax.all_gather(weight, "dp", axis=0, tiled=True)
        columns = whole.shape[1]
        return self.mine(whole.reshape(self.width, self.seq_count, -1, columns), 1).reshape(-1, columns)

    def gate_up(self, weight):
        rows = weight.shape[0]
        block = self.mine(weight.reshape(rows, 2, self.seq_count, -1), 2).reshape(rows, -1)
        return lax.all_gather(block, "dp", axis=0, tiled=True)

    def down(self, weight):
        whole = lax.all_gather(weight, "dp", axis=0, tiled=True)
        return self.mine(whole.reshape(self.seq_count, -1, whole.shape[1]), 0)

    def scatter(self, grad):
        return lax.psum_scatter(grad.astype(LOW), "dp", scatter_dimension=0, tiled=True)

    def both(self, grad):
        return lax.psum(self.scatter(grad), "seq").astype(WIDE)

    def grad_down(self, grad):
        return self.both(self.spread(grad, 0).reshape(-1, grad.shape[1]))

    def grad_out(self, grad):
        columns = grad.shape[1]
        return self.both(self.spread(grad.reshape(self.width, -1, columns), 1).reshape(-1, columns))

    def grad_columns(self, grad, blocks):
        total = self.scatter(grad)
        rows = total.shape[0]
        pieces = lax.all_gather(total.reshape(rows, blocks, -1), "seq", axis=2)
        return pieces.reshape(rows, -1).astype(WIDE)

    def grad_gate_up(self, grad):
        return self.grad_columns(grad, 2)

    def grad_proj(self, grad):
        return self.grad_columns(grad, 4 * self.width)

    def grad_decay(self, grad):
        return self.grad_columns(grad, self.width)

    def head_columns(self, table):
        return self.mine(table.reshape(table.shape[:-1] + (self.width, self.seq_count)), table.ndim)


def rms(value):
    return lax.rsqrt(jnp.mean(value * value, axis=1, keepdims=True) + 1e-06)


def norm_back(grad_normed, source, inverse, gain):
    grad_gain = jnp.sum(grad_normed * source * inverse, axis=0)
    scaled = grad_normed * gain
    grad_source = inverse * (
        scaled - source * inverse * inverse * jnp.mean(scaled * source, axis=1, keepdims=True)
    )
    return (grad_source, grad_gain)


def split_heads(matrix, count):
    return matrix.reshape(matrix.shape[0], count, -1).transpose(1, 0, 2)


def join_heads(tensor):
    return tensor.transpose(1, 0, 2).reshape(tensor.shape[1], -1)


def shards(
    inputs, segments, valid_count, teacher, cotangent, w_proj, w_decay, b_decay, w_out,
    gain_ret, gain_ffn, w_gu, w_down,
):
    dp_count, seq_count = lax.axis_size("dp"), lax.axis_size("seq")
    tokens = inputs[0]
    count, model_width = tokens.shape
    heads = w_decay.shape[1]
    head_dim = model_width // heads
    hidden = w_down.shape[0] * dp_count
    me_seq = lax.axis_index("seq")
    placed = dp_count == 8 and seq_count == 4 and heads == 16
    if placed:
        links = Links(dp_count, seq_count)
        plan = Placed(links, heads, hidden)

        def tokens_in(value):
            return jnp.concatenate(links.tokens_in(value), axis=0)

        def tokens_out(value):
            return links.tokens_out(jnp.split(value, seq_count, axis=0))

        def in_order(value):
            return blocks_at(value, [me_seq ^ k for k in range(seq_count)], count, 0)

        out_order = in_order
    else:
        plan = Plain(dp_count, seq_count, heads, hidden)

        def tokens_in(value):
            return lax.all_gather(value, "seq", axis=0, tiled=True)

        def tokens_out(value):
            return lax.psum_scatter(
                value.astype(LOW), "seq", scatter_dimension=0, tiled=True
            ).astype(WIDE)

        def in_order(value):
            return value

        out_order = in_order
    width = heads // seq_count

    scale_one = rms(tokens)
    normed_here = plan.to_rel((tokens * scale_one * gain_ret).astype(LOW))
    normed = in_order(tokens_in(normed_here))
    row_segments = in_order(tokens_in(jnp.broadcast_to(segments[0][:, None], (count, 128))))[:, 0]
    decay_w = plan.decay(w_decay)
    proj_w = plan.proj(w_proj)
    out_w = plan.out(w_out)
    gu_w = plan.gate_up(w_gu)
    down_w = plan.down(w_down)
    units = plan.units
    row = normed.shape[0]

    own_decay_w = plan.head_columns(decay_w)
    decay_logit = dot(normed, own_decay_w) + plan.head_columns(b_decay)
    cumulative = jnp.cumsum(jax.nn.log_sigmoid(decay_logit) / 16.0, axis=0).T
    projected = dot(normed, proj_w)
    share = width * head_dim
    queries = split_heads((projected[:, :share] * head_dim ** (-0.5)).astype(LOW), width)
    key_rows = split_heads(projected[:, share : 2 * share].astype(LOW), width)
    values = split_heads(projected[:, 2 * share : 3 * share].astype(LOW), width)
    outgate = projected[:, 3 * share :]
    order = jnp.arange(row, dtype=jnp.int32)
    allowed = (row_segments[:, None] == row_segments[None, :]) & (order[:, None] >= order[None, :])
    spread = cumulative[:, :, None] - cumulative[:, None, :]
    table = jnp.where(allowed[None], jnp.exp(jnp.where(allowed[None], spread, 0.0)), 0.0)
    scores = batch_dot(queries, key_rows, 2, 2) * table
    retained = batch_dot(scores.astype(LOW), values, 2, 1)
    power = jnp.mean(retained * retained, axis=2, keepdims=True)
    inverse = lax.rsqrt(jnp.maximum(power, 1.0))
    unit = retained * inverse
    gate_heads = split_heads(outgate, width)
    gate_sigma = jax.nn.sigmoid(gate_heads)
    gated = join_heads((gate_heads * gate_sigma * unit).astype(LOW))
    mixed = tokens + tokens_out(out_order(dot(gated, out_w)))

    scale_two = rms(mixed)
    normed_ffn = tokens_in(plan.to_rel((mixed * scale_two * gain_ffn).astype(LOW)))
    gate_up = dot(normed_ffn, gu_w)
    gate_part, up_part = gate_up[:, :units], gate_up[:, units:]
    sigma = jax.nn.sigmoid(gate_part)
    activated = (gate_part * sigma * up_part).astype(LOW)
    result = mixed + tokens_out(dot(activated, down_w))

    position = me_seq * count + jnp.arange(count, dtype=jnp.int32)
    valid_mask = (position < valid_count[0]).astype(WIDE)[:, None]
    mismatch = result - teacher[0]
    grad_out = cotangent[0] + valid_mask * mismatch
    squared_local = jnp.sum(valid_mask * mismatch * mismatch)
    count_local = jnp.sum(valid_mask)

    grad_ffn = tokens_in(grad_out.astype(LOW))
    down_grad = plan.grad_down(dot(activated, grad_ffn, 0, 0).astype(LOW))
    grad_act = dot(grad_ffn, down_w, 1, 1)
    grad_gate = grad_act * up_part * sigma * (1.0 + gate_part * (1.0 - sigma))
    grad_up = grad_act * gate_part * sigma
    grad_both = jnp.concatenate([grad_gate, grad_up], axis=1).astype(LOW)
    gu_grad = plan.grad_gate_up(dot(normed_ffn, grad_both, 0, 0).astype(LOW))
    grad_normed = plan.from_rel(tokens_out(dot(grad_both, gu_w, 1, 1)))
    grad_mid, gain_ffn_grad = norm_back(grad_normed, mixed, scale_two, gain_ffn)
    grad_mixed = grad_out + grad_mid

    grad_att = in_order(tokens_in(grad_mixed.astype(LOW)))
    out_grad = plan.grad_out(dot(gated, grad_att, 0, 0).astype(LOW))
    grad_gated = split_heads(dot(grad_att, out_w, 1, 1), width)
    grad_outgate = grad_gated * unit * gate_sigma * (1.0 + gate_heads * (1.0 - gate_sigma))
    grad_unit = grad_gated * gate_heads * gate_sigma
    along = jnp.mean(grad_unit * unit, axis=2, keepdims=True)
    grad_retained = inverse * jnp.where(power > 1.0, grad_unit - unit * along, grad_unit)
    grad_low = grad_retained.astype(LOW)
    grad_scores = batch_dot(grad_low, values, 2, 2)
    energy = scores * grad_scores
    grad_pairs = (table * grad_scores).astype(LOW)
    grad_q = batch_dot(grad_pairs, key_rows, 2, 1)
    grad_k = batch_dot(grad_pairs, queries, 1, 1)
    grad_v = batch_dot(scores.astype(LOW), grad_low, 1, 1)
    grad_cum = (jnp.sum(energy, axis=2) - jnp.sum(energy, axis=1)).T
    grad_logdecay = lax.cumsum(grad_cum, axis=0, reverse=True)
    grad_logit = grad_logdecay * jax.nn.sigmoid(-decay_logit) / 16.0
    bias_local = jnp.sum(grad_logit, axis=0)
    grad_logit_low = grad_logit.astype(LOW)
    grad_proj = jnp.concatenate(
        [
            join_heads(part)
            for part in (grad_q * head_dim ** (-0.5), grad_k, grad_v, grad_outgate)
        ],
        axis=1,
    ).astype(LOW)
    proj_grad = plan.grad_proj(dot(normed, grad_proj, 0, 0).astype(LOW))
    decay_grad = plan.grad_decay(dot(normed, grad_logit_low, 0, 0))
    back = dot(grad_proj, proj_w, 1, 1) + dot(grad_logit_low, own_decay_w, 1, 1)
    grad_normed_one = plan.from_rel(tokens_out(out_order(back)))
    grad_first, gain_ret_grad = norm_back(grad_normed_one, tokens, scale_one, gain_ret)
    grad_tokens = grad_mixed + grad_first

    bias_wide = jnp.stack(
        [jnp.where(me_seq == s, bias_local, 0.0) for s in range(seq_count)], axis=1
    ).reshape(heads)
    totals = lax.psum(
        (gain_ret_grad, gain_ffn_grad, bias_wide, squared_local, count_local), ("dp", "seq")
    )
    mse = totals[3] / (totals[4] * model_width)
    return (
        result[None],
        grad_tokens[None],
        proj_grad,
        decay_grad,
        totals[2],
        out_grad,
        totals[0],
        totals[1],
        gu_grad,
        down_grad,
        mse,
    )


def solution(mesh):
    rows = P("dp", None)
    in_specs = (
        P("dp", "seq", None),
        P("dp", "seq"),
        P("dp"),
        P("dp", "seq", None),
        P("dp", "seq", None),
        rows,
        rows,
        P(),
        rows,
        P(),
        P(),
        rows,
        rows,
    )
    out_specs = (
        P("dp", "seq", None),
        P("dp", "seq", None),
        rows,
        rows,
        P(),
        rows,
        P(),
        P(),
        rows,
        rows,
        P(),
    )
    return jax.shard_map(shards, mesh=mesh, in_specs=in_specs, out_specs=out_specs, check_vma=False)
```

```python
import functools

import jax
import jax.numpy as jnp
from jax import lax
from jax.experimental import pallas as pl
from jax.experimental.pallas import tpu as pltpu
from jax.sharding import PartitionSpec as P

LOW = jnp.bfloat16
WIDE = jnp.float32
ORDER = (2, 1, 3, 0)
EXTRA = 128
VMEM_BYTES = 56 * 1024 * 1024


def dot(left, right, left_dim=1, right_dim=0):
    return lax.dot_general(
        left, right, (((left_dim,), (right_dim,)), ((), ())), preferred_element_type=WIDE
    )


def blocks_at(matrix, places, size, axis):
    return jnp.concatenate(
        [lax.dynamic_slice_in_dim(matrix, place * size, size, axis) for place in places], axis=axis
    )


def after(value, *tokens):
    return lax.optimization_barrier((value,) + tokens)[0]


def in_vmem():
    return pl.BlockSpec(memory_space=pltpu.VMEM)


def anywhere():
    return pl.BlockSpec(memory_space=pl.ANY)


def cost(*unused):
    return pl.CostEstimate(flops=0, bytes_accessed=0, transcendentals=0)


def pieces_kernel(*refs):
    rows, pieces, target = refs[0], refs[1:-1], refs[-1]
    target[...] = dot(rows[...], jnp.concatenate([piece[...] for piece in pieces], axis=0))


def pieces_product(rows, pieces):
    depth, width = pieces[0].shape
    height, count, tile = rows.shape[0], len(pieces), 256
    return pl.pallas_call(
        pieces_kernel,
        grid=(-(-width // tile),),
        in_specs=[pl.BlockSpec((height, count * depth), lambda i: (0, 0))]
        + [pl.BlockSpec((depth, tile), lambda i: (0, i))] * count,
        out_specs=pl.BlockSpec((height, tile), lambda i: (0, i)),
        out_shape=jax.ShapeDtypeStruct((height, width), WIDE),
        compiler_params=pltpu.CompilerParams(vmem_limit_bytes=VMEM_BYTES),
        cost_estimate=cost(),
    )(rows, *pieces)


def gate_up_kernel(count, *refs):
    rows, gate_w, up_w = refs[0], refs[1 : 1 + count], refs[1 + count : 1 + 2 * count]
    gate, up, activated = refs[1 + 2 * count :]
    tile = gate.shape[1]
    left = jnp.concatenate([piece[...] for piece in gate_w], axis=0)
    right = jnp.concatenate([piece[...] for piece in up_w], axis=0)
    both = dot(rows[...], jnp.concatenate([left, right], axis=1))
    gate_part, up_part = both[:, :tile], both[:, tile:]
    gate[...] = gate_part
    up[...] = up_part
    activated[...] = (gate_part * jax.nn.sigmoid(gate_part) * up_part).astype(LOW)


def gate_up_product(rows, pieces, units):
    height, depth = rows.shape
    tile = 128
    steps, count = units // tile, len(pieces)
    column = pl.BlockSpec((height, tile), lambda i: (0, i))
    size = pieces[0].shape[0]
    return pl.pallas_call(
        functools.partial(gate_up_kernel, count),
        grid=(steps,),
        in_specs=[pl.BlockSpec((height, depth), lambda i: (0, 0))]
        + [pl.BlockSpec((size, tile), lambda i: (0, i))] * count
        + [pl.BlockSpec((size, tile), lambda i: (0, steps + i))] * count,
        out_specs=[column] * 3,
        out_shape=[
            jax.ShapeDtypeStruct((height, units), WIDE),
            jax.ShapeDtypeStruct((height, units), WIDE),
            jax.ShapeDtypeStruct((height, units), LOW),
        ],
        compiler_params=pltpu.CompilerParams(vmem_limit_bytes=VMEM_BYTES),
        cost_estimate=cost(),
    )(rows, *pieces, *pieces)


def in_row_order_kernel(*refs):
    pieces, target = refs[:-1], refs[-1]
    me = lax.axis_index("seq")
    size = pieces[0].shape[0]
    for k, piece in enumerate(pieces):
        target[pl.ds(pl.multiple_of(lax.bitwise_xor(me, k) * size, size), size), :] = piece[...]


def in_row_order(pieces):
    size, width = pieces[0].shape
    return pl.pallas_call(
        in_row_order_kernel,
        in_specs=[in_vmem()] * len(pieces),
        out_specs=in_vmem(),
        out_shape=jax.ShapeDtypeStruct((len(pieces) * size, width), LOW),
        compiler_params=pltpu.CompilerParams(vmem_limit_bytes=VMEM_BYTES),
        cost_estimate=cost(),
    )(*pieces)


def proj_share_kernel(blocks, seq_count, source, decay, target):
    me = lax.axis_index("seq")
    rows, extra = decay.shape
    size = (target.shape[1] - EXTRA) // blocks
    for i in range(blocks):
        place = pl.multiple_of((i * seq_count + me) * size, size)
        target[:, i * size : (i + 1) * size] = source[:, pl.ds(place, size)]
    padded = jnp.concatenate([decay[...], jnp.zeros((rows, EXTRA - extra), LOW)], axis=1)
    target[:, blocks * size :] = padded


def row_shares_kernel(part, shard, seq_count, out, down, out_to, down_to):
    me = lax.axis_index("seq")
    half = out_to.shape[0]
    out_to[...] = out[pl.ds(pl.multiple_of(lax.rem(me, 2) * half, half), half), :]
    sure = shard - part * (seq_count - 1)
    rest = part - sure
    start = pl.multiple_of(me * part, 16)
    down_to[:sure, :] = down[pl.ds(start, sure), :]
    if rest:
        last = pl.multiple_of(jnp.minimum(start + sure, shard - rest), 16)
        rows = down[pl.ds(last, rest), :]
        down_to[sure:, :] = jnp.where(me < seq_count - 1, rows, jnp.zeros_like(rows))


def gate_up_share_kernel(part, shard, dp_count, source, target):
    me = lax.axis_index("seq")
    lane = 128
    window = 384
    columns = source.shape[1]
    half = dp_count * part
    row = lax.broadcasted_iota(jnp.int32, (window, lane), 0)
    col = lax.broadcasted_iota(jnp.int32, (window, lane), 1)
    for tile in range(target.shape[1] // lane):
        first = tile * lane % half
        which = tile * lane // half
        total = None
        for d in range(first // part, (first + lane - 1) // part + 1):
            base = (which * dp_count + d) * shard + me * part
            begin = pl.multiple_of(
                jnp.minimum(lax.div(base, lane) * lane, (columns - window) // lane * lane), lane
            )
            unit = first + col - d * part
            hit = (row + begin == base + unit) & (unit >= 0) & (unit < part)
            hit = hit & (me * part + unit < shard)
            chosen = jnp.where(hit, 1.0, 0.0).astype(LOW)
            piece = jnp.dot(source[:, pl.ds(begin, window)], chosen, preferred_element_type=WIDE)
            total = piece if total is None else total + piece
        target[:, pl.ds(tile * lane, lane)] = total.astype(LOW)


def gate_up_whole_kernel(part, shard, *refs):
    pieces, target, held = refs[:-2], refs[-2], refs[-1]
    me = lax.axis_index("seq")
    lane, window = 128, 256
    count = len(pieces)
    for k in range(count):
        place = lax.bitwise_xor(me, k)
        held[place] = pieces[k][...]
    row = lax.broadcasted_iota(jnp.int32, (window, lane), 0)
    col = lax.broadcasted_iota(jnp.int32, (window, lane), 1)
    width = pieces[0].shape[1]
    for tile in range(target.shape[1] // lane):
        at = tile * lane
        total = None
        while at < (tile + 1) * lane:
            block, inside = divmod(at, shard)
            share, unit = divmod(inside, part)
            stop = min((tile + 1) * lane, block * shard + min((share + 1) * part, shard))
            from_column = block * part + unit
            begin = min(from_column // lane * lane, width - window)
            off = at - tile * lane
            hit = (row + begin - from_column == col - off) & (col >= off) & (col < off + stop - at)
            chosen = jnp.where(hit, 1.0, 0.0).astype(LOW)
            piece = jnp.dot(held[share, :, begin : begin + window], chosen, preferred_element_type=WIDE)
            total = piece if total is None else total + piece
            at = stop
        target[:, tile * lane : (tile + 1) * lane] = total


def proj_whole_kernel(skip, *refs):
    pieces, target = refs[skip:-1], refs[-1]
    me = lax.axis_index("seq")
    size = pieces[0].shape[1]
    for k, piece in enumerate(pieces):
        place = pl.multiple_of(lax.bitwise_xor(me, k) * size, size)
        target[:, pl.ds(place, size)] = piece[...].astype(WIDE)


def down_whole_kernel(part, shard, *refs):
    pieces, target = refs[:-1], refs[-1]
    me = lax.axis_index("seq")
    count = len(pieces)
    sure = shard - part * (count - 1)
    for k, piece in enumerate(pieces):
        place = lax.bitwise_xor(me, k)
        start = pl.multiple_of(place * part, 16)
        target[pl.ds(start, sure), :] = piece[:sure, :].astype(WIDE)
        if sure < part:

            @pl.when(place < count - 1)
            def _(piece=piece, start=start):
                target[pl.ds(pl.multiple_of(start + sure, 16), part - sure), :] = piece[sure:, :].astype(WIDE)


def triangle(size, reverse):
    row = lax.broadcasted_iota(jnp.int32, (size, size), 0)
    col = lax.broadcasted_iota(jnp.int32, (size, size), 1)
    return jnp.where(row <= col if reverse else row >= col, 1.0, 0.0)


def running_sum(table, step, source, target, reverse):
    count, lanes = source.shape
    carry = jnp.zeros((1, lanes), WIDE)
    starts = range(0, count, step)
    for at in reversed(starts) if reverse else starts:
        block = source[at : at + step, :]
        sums = lax.dot_general(
            table, block, (((1,), (0,)), ((), ())),
            precision=lax.Precision.HIGHEST, preferred_element_type=WIDE,
        ) + carry
        target[at : at + step, :] = sums
        carry = carry + jnp.sum(block, axis=0, keepdims=True)


def decay_rows(at, size, cum_col, cum_row, seg_col, seg_row):
    wide = at + size
    spread = cum_col[at:wide] - cum_row[:, :wide]
    order_t = lax.broadcasted_iota(jnp.int32, (size, wide), 0) + at
    order_s = lax.broadcasted_iota(jnp.int32, (size, wide), 1)
    allowed = (seg_col[at:wide] == seg_row[:, :wide]) & (order_t >= order_s)
    return jnp.where(allowed, jnp.exp(jnp.minimum(spread, 0.0)), 0.0)


def lane_of(table, lane):
    lanes = lax.broadcasted_iota(jnp.int32, table.shape, 1)
    return jnp.sum(jnp.where(lanes == lane, table, 0.0), axis=1, keepdims=True)


def forward_kernel(
    step, scale, seq_count, q, k, v, gate, logit, bias, seg_col, seg_row, gated, kept, cum, cum_rows, held
):
    head = pl.program_id(0)
    lane = head * seq_count + lax.axis_index("seq")

    @pl.when(head == 0)
    def _():
        value = logit[...] + bias[...]
        held[...] = (jnp.minimum(value, 0.0) - jnp.log1p(jnp.exp(-jnp.abs(value)))) / 16.0
        running_sum(triangle(step, False), step, held, cum, False)
        cum_rows[...] = cum[...].T

    keys, values = k[...].astype(LOW), v[...].astype(LOW)
    seg_c, seg_r = seg_col[...], seg_row[...]
    cum_c, cum_r = lane_of(cum[...], lane), cum_rows[pl.ds(lane, 1), :]
    for at in range(0, q.shape[0], step):
        stop = at + step
        rows = (q[at:stop, :] * scale).astype(LOW)
        scores = dot(rows, keys[:stop], 1, 1) * decay_rows(at, step, cum_c, cum_r, seg_c, seg_r)
        high = scores.astype(LOW)
        rest = (scores - high.astype(WIDE)).astype(LOW)
        retained = dot(high, values[:stop]) + dot(rest, values[:stop])
        kept[at:stop, :] = retained
        power = jnp.mean(retained * retained, axis=1, keepdims=True)
        unit = retained * lax.rsqrt(jnp.maximum(power, 1.0))
        gates = gate[at:stop, :]
        gated[at:stop, :] = (gates * jax.nn.sigmoid(gates) * unit).astype(LOW)


def backward_kernel(
    step, scale, width, seq_count, q, k, v, gate, logit, bias, kept, grad, cum, cum_rows, seg_col, seg_row,
    grad_proj, bias_sum, grad_k, grad_v, grad_cum, held,
):
    head = pl.program_id(0)
    lane = head * seq_count + lax.axis_index("seq")
    size = q.shape[1]
    keys, values = k[...].astype(LOW), v[...].astype(LOW)
    seg_c, seg_r = seg_col[...], seg_row[...]
    cum_c, cum_r = lane_of(cum[...], lane), cum_rows[pl.ds(lane, 1), :]

    def columns(block):
        return pl.ds(pl.multiple_of((block * width + head) * size, size), size)

    @pl.when(head == 0)
    def _():
        grad_cum[...] = jnp.zeros_like(grad_cum)

    count = q.shape[0]
    lanes = lax.broadcasted_iota(jnp.int32, (step, EXTRA), 1)
    for at in reversed(range(0, count, step)):
        stop = at + step
        first = stop == count
        retained, gates, grads = kept[at:stop, :], gate[at:stop, :], grad[at:stop, :]
        power = jnp.mean(retained * retained, axis=1, keepdims=True)
        inverse = lax.rsqrt(jnp.maximum(power, 1.0))
        unit = retained * inverse
        sigma = jax.nn.sigmoid(gates)
        grad_proj[at:stop, columns(3)] = (
            grads * unit * sigma * (1.0 + gates * (1.0 - sigma))
        ).astype(LOW)
        grad_unit = grads * gates * sigma
        along = jnp.mean(grad_unit * unit, axis=1, keepdims=True)
        grad_low = (inverse * jnp.where(power > 1.0, grad_unit - unit * along, grad_unit)).astype(LOW)
        rows = (q[at:stop, :] * scale).astype(LOW)
        table = decay_rows(at, step, cum_c, cum_r, seg_c, seg_r)
        scores = (dot(rows, keys[:stop], 1, 1) * table).astype(LOW)
        pairs = (table * dot(grad_low, values[:stop], 1, 1)).astype(LOW)
        grad_q = dot(pairs, keys[:stop])
        grad_proj[at:stop, columns(0)] = (grad_q * scale).astype(LOW)
        part_k = dot(pairs, rows, 0, 0)
        part_v = dot(scores, grad_low, 0, 0)
        if first:
            grad_k[:stop, :] = part_k
            grad_v[:stop, :] = part_v
        else:
            grad_k[:stop, :] += part_k
            grad_v[:stop, :] += part_v
        along_q = jnp.sum(rows.astype(WIDE) * grad_q, axis=1, keepdims=True)
        along_k = jnp.sum(keys[at:stop].astype(WIDE) * grad_k[at:stop, :], axis=1, keepdims=True)
        grad_cum[at:stop, :] += jnp.where(lanes == lane, along_q - along_k, 0.0)
    grad_proj[:, columns(1)] = grad_k[...].astype(LOW)
    grad_proj[:, columns(2)] = grad_v[...].astype(LOW)

    @pl.when(head == width - 1)
    def _():
        running_sum(triangle(step, True), step, grad_cum, held, True)
        value = held[...] * jax.nn.sigmoid(-(logit[...] + bias[...])) / 16.0
        bias_sum[...] = jnp.sum(value, axis=0, keepdims=True)
        grad_proj[:, 4 * width * size :] = value.astype(LOW)


def head_specs(row, size, width):
    def block(number):
        return pl.BlockSpec((row, size), lambda h: (0, number * width + h))

    def same(shape):
        return pl.BlockSpec(shape, lambda h: (0, 0))

    logit = pl.BlockSpec((row, EXTRA), lambda h: (0, 4 * width * size // EXTRA))
    return block, same, logit


def retention(projected, bias, seg_col, seg_row, width, size):
    row = projected.shape[0]
    block, same, logit = head_specs(row, size, width)
    pairs = row * row * width * 5 // 8
    return pl.pallas_call(
        functools.partial(forward_kernel, row // 4, size ** (-0.5), lax.axis_size("seq")),
        grid=(width,),
        in_specs=[block(0), block(1), block(2), block(3), logit, same((1, EXTRA)), same((row, 1)), same((1, row))],
        out_specs=[block(0), block(0), same((row, EXTRA)), same((EXTRA, row))],
        out_shape=[
            jax.ShapeDtypeStruct((row, width * size), LOW),
            jax.ShapeDtypeStruct((row, width * size), WIDE),
            jax.ShapeDtypeStruct((row, EXTRA), WIDE),
            jax.ShapeDtypeStruct((EXTRA, row), WIDE),
        ],
        scratch_shapes=[pltpu.VMEM((row, EXTRA), WIDE)],
        compiler_params=pltpu.CompilerParams(vmem_limit_bytes=VMEM_BYTES),
        cost_estimate=cost(pairs * size * 4, projected.size * 6, pairs),
    )(*([projected] * 5), bias, seg_col, seg_row)


def retention_back(projected, bias, kept, grad_gated, cum, cum_rows, seg_col, seg_row, width, size):
    row = projected.shape[0]
    block, same, logit = head_specs(row, size, width)
    pairs = row * row * width * 5 // 8
    return pl.pallas_call(
        functools.partial(backward_kernel, row // 4, size ** (-0.5), width, lax.axis_size("seq")),
        grid=(width,),
        in_specs=[block(0), block(1), block(2), block(3), logit, same((1, EXTRA)), block(0), block(0)]
        + [same((row, EXTRA)), same((EXTRA, row)), same((row, 1)), same((1, row))],
        out_specs=[same((row, 4 * width * size + EXTRA)), same((1, EXTRA))],
        out_shape=[
            jax.ShapeDtypeStruct((row, 4 * width * size + EXTRA), LOW),
            jax.ShapeDtypeStruct((1, EXTRA), WIDE),
        ],
        scratch_shapes=[pltpu.VMEM((row, size), WIDE)] * 2 + [pltpu.VMEM((row, EXTRA), WIDE)] * 2,
        compiler_params=pltpu.CompilerParams(vmem_limit_bytes=VMEM_BYTES),
        cost_estimate=cost(pairs * size * 10, projected.size * 8, pairs),
    )(*([projected] * 5), bias, kept, grad_gated, cum, cum_rows, seg_col, seg_row)


class Order:
    def __init__(self):
        self.last = None

    def put(self, value):
        if self.last is not None:
            value = after(value, self.last)
        self.last = value
        return value


class Links:
    def __init__(self, dp_count, seq_count):
        self.dp_count, self.seq_count = dp_count, seq_count
        self.ring = dp_count // 2
        self.me_dp, self.me_seq = lax.axis_index("dp"), lax.axis_index("seq")
        self.turn, self.side = self.me_dp // 2, self.me_dp % 2

    def around(self, value, by=1):
        count = self.dp_count
        return lax.ppermute(value, "dp", [(d, (d + 2 * by) % count) for d in range(count)])

    def across(self, value):
        return lax.ppermute(value, "dp", [(d, d ^ 1) for d in range(self.dp_count)])

    def across_one_way(self, value, toward):
        pairs = [
            (d * self.seq_count + s, (d ^ 1) * self.seq_count + s)
            for d in range(self.dp_count)
            for s in range(self.seq_count)
            if (d % 2 == s // 2) != toward
        ]
        return lax.ppermute(value, ("dp", "seq"), pairs)

    def core(self, value):
        return lax.ppermute(value, "seq", [(s, s ^ 1) for s in range(self.seq_count)])

    def chip(self, value):
        return lax.ppermute(value, "seq", [(s, s ^ 2) for s in range(self.seq_count)])

    def sources(self):
        return [
            ((self.turn - r) % self.ring) * 2 + (self.side ^ e) for e in range(2) for r in ORDER
        ]

    def spot(self, r):
        found = ORDER.index(0)
        for value in range(1, self.ring):
            found = jnp.where(r == value, ORDER.index(value), found)
        return found

    def places(self):
        found = []
        for d in range(self.dp_count):
            r = (self.turn - d // 2) % self.ring
            found.append(self.spot(r) + (self.side ^ (d % 2)) * self.ring)
        return found

    def total_steps(self):
        def step(axis, count, apart):
            pairs = [(d, d ^ apart) for d in range(count)]
            return lambda value: value + lax.ppermute(value, axis, pairs)

        return [step("seq", self.seq_count, apart) for apart in (1, 2)] + [
            step("dp", self.dp_count, apart) for apart in (1, 2, 4)
        ]

    def own_order(self, rows):
        me = self.me_seq
        return blocks_at(rows, [me ^ 1, me ^ 3, me ^ 2, me], rows.shape[0] // 4, 0)

    def to_rel(self, value):
        return blocks_at(value, self.sources(), value.shape[1] // self.dp_count, 1)

    def from_rel(self, value):
        return blocks_at(value, self.places(), value.shape[1] // self.dp_count, 1)


def sum_low(*parts):
    total = parts[0].astype(WIDE)
    for part in parts[1:]:
        total = total + part.astype(WIDE)
    return total.astype(LOW)


def weight_shares(links, width, part, shard, w_proj, w_decay, w_out, w_down):
    rows, columns = w_proj.shape[0], w_proj.shape[1] // links.seq_count + EXTRA
    model = w_down.shape[1]
    block = min(rows, 64)
    proj = pl.pallas_call(
        functools.partial(proj_share_kernel, 4 * width, links.seq_count),
        grid=(rows // block,),
        in_specs=[
            pl.BlockSpec((block, w_proj.shape[1]), lambda i: (i, 0)),
            pl.BlockSpec((block, w_decay.shape[1]), lambda i: (i, 0)),
        ],
        out_specs=pl.BlockSpec((block, columns), lambda i: (i, 0)),
        out_shape=jax.ShapeDtypeStruct((rows, columns), LOW),
        compiler_params=pltpu.CompilerParams(vmem_limit_bytes=VMEM_BYTES),
        cost_estimate=cost(0, 10 * rows * columns),
    )(w_proj, w_decay)
    out, down = pl.pallas_call(
        functools.partial(row_shares_kernel, part, shard, links.seq_count),
        in_specs=[in_vmem()] * 2,
        out_specs=[in_vmem()] * 2,
        out_shape=[
            jax.ShapeDtypeStruct((w_out.shape[0] // 2, model), LOW),
            jax.ShapeDtypeStruct((part, model), LOW),
        ],
        compiler_params=pltpu.CompilerParams(vmem_limit_bytes=VMEM_BYTES),
        cost_estimate=cost(0, 3 * w_out.size + 3 * w_down.size),
    )(w_out, w_down)
    return proj, out, down


def gate_up_share(links, part, shard, w_gu):
    rows, units = w_gu.shape[0], part * links.dp_count
    return pl.pallas_call(
        functools.partial(gate_up_share_kernel, part, shard, links.dp_count),
        in_specs=[in_vmem()],
        out_specs=in_vmem(),
        out_shape=jax.ShapeDtypeStruct((rows, 2 * units), LOW),
        compiler_params=pltpu.CompilerParams(vmem_limit_bytes=VMEM_BYTES),
        cost_estimate=cost(2 * rows * 768 * 2 * units, 2 * w_gu.size + 4 * rows * units),
    )(w_gu)


def whole_down(part, shard, pieces):
    model = pieces[0].shape[1]
    return pl.pallas_call(
        functools.partial(down_whole_kernel, part, shard),
        in_specs=[in_vmem()] * 4,
        out_specs=in_vmem(),
        out_shape=jax.ShapeDtypeStruct((shard, model), WIDE),
        compiler_params=pltpu.CompilerParams(vmem_limit_bytes=VMEM_BYTES),
        cost_estimate=cost(0, 6 * shard * model),
    )(*pieces)


def whole_gate_up(part, shard, dp_count, pieces):
    rows, columns = pieces[0].shape
    block = min(rows, 64)
    whole = 2 * dp_count * shard
    return pl.pallas_call(
        functools.partial(gate_up_whole_kernel, part, shard),
        grid=(rows // block,),
        in_specs=[pl.BlockSpec((block, columns), lambda i: (i, 0))] * 4,
        out_specs=pl.BlockSpec((block, whole), lambda i: (i, 0)),
        out_shape=jax.ShapeDtypeStruct((rows, whole), WIDE),
        scratch_shapes=[pltpu.VMEM((4, block, columns), LOW)],
        compiler_params=pltpu.CompilerParams(vmem_limit_bytes=VMEM_BYTES),
        cost_estimate=cost(rows * whole * 1024, rows * whole * 6),
    )(*pieces)


def whole_proj(half, number, size, kept, pieces):
    rows = pieces[0].shape[0]
    return pl.pallas_call(
        functools.partial(proj_whole_kernel, len(kept)),
        grid=(half,),
        in_specs=[anywhere()] * len(kept) + [pl.BlockSpec((rows, size), lambda i: (0, i))] * 4,
        out_specs=pl.BlockSpec((rows, 4 * size), lambda i: (0, number * half + i)),
        out_shape=jax.ShapeDtypeStruct((rows, 8 * half * size), WIDE),
        input_output_aliases={0: 0} if kept else {},
        compiler_params=pltpu.CompilerParams(vmem_limit_bytes=VMEM_BYTES),
        cost_estimate=cost(0, rows * half * size * 24),
    )(*kept, *pieces)


def placed_shards(
    inputs, segments, valid_count, teacher, cotangent, w_proj, w_decay, b_decay, w_out,
    gain_ret, gain_ffn, w_gu, w_down,
):
    dp_count, seq_count = lax.axis_size("dp"), lax.axis_size("seq")
    links, order = Links(dp_count, seq_count), Order()
    put = order.put
    tokens = inputs[0]
    count, model_width = tokens.shape
    heads = w_decay.shape[1]
    head_dim = model_width // heads
    width = heads // seq_count
    shard = w_down.shape[0]
    part = -(-shard // (16 * seq_count)) * 16
    units = part * dp_count
    first_core, x_half = links.me_seq % 2 == 0, links.me_seq // 2

    proj_share, out_share, down_share = weight_shares(
        links, width, part, shard, w_proj, w_decay, w_out, w_down
    )
    proj_share = put(proj_share)
    p_ring = links.around(proj_share)
    p_0 = links.across(proj_share)
    scale_one = rms(tokens)
    normed_here = links.to_rel((tokens * scale_one * gain_ret).astype(LOW))
    ids = jnp.broadcast_to(segments[0][:, None].astype(LOW), (count, EXTRA))
    sent = put(jnp.concatenate([normed_here, ids], axis=1))
    n_far, n_near = links.chip(sent), links.core(sent)
    out_share, down_share = put(out_share), put(down_share)
    out_cross = links.across_one_way(out_share, False)
    gu_share = put(gate_up_share(links, part, shard, after(w_gu, sent)))
    p_own_1, p_0 = put(p_ring), put(p_0)
    p_ring, p_1 = links.around(p_own_1), links.across(p_own_1)
    n_near, n_far = put(n_near), put(n_far)
    n_both = put(links.core(n_far))
    normed = put(in_row_order([sent, n_near, n_far, n_both]))
    seg_col = normed[:, model_width : model_width + 1].astype(jnp.int32)
    out_block = put(jnp.where(links.side == x_half, out_share, put(out_cross)))
    p_own_2 = put(p_ring)
    p_ring = links.around(p_own_2)
    p_1 = put(p_1)
    p_2 = links.across(p_own_2)
    p_own_3 = put(p_ring)
    o_ring = links.around(out_block)
    p_2 = put(p_2)
    p_3 = links.across(p_own_3)
    o_own_1 = put(o_ring)
    o_ring = links.around(o_own_1)
    o_own_2 = put(o_ring)
    g_ring = links.around(put(gu_share))
    o_ring = links.around(o_own_2)
    p_3 = put(p_3)
    g_0 = links.across(put(gu_share))
    p_pieces = [p_own_2, p_own_1, p_own_3, proj_share, p_2, p_1, p_3, p_0]
    projected = put(pieces_product(normed, p_pieces))
    bias = jnp.pad(b_decay, (0, EXTRA - heads))[None]
    gated, kept, cum, cum_rows = retention(projected, bias, seg_col, seg_col.T, width, head_dim)
    gated = put(gated)
    o_own_3 = put(o_ring)
    out_w = blocks_at(
        jnp.concatenate([o_own_2, o_own_1, o_own_3, out_block], axis=0),
        [links.spot((links.turn - j) % links.ring) for j in range(links.ring)],
        out_share.shape[0],
        0,
    )

    def tokens_start(rows, weight, dims):
        come = links.core(put(dot(rows[: 2 * count], weight, *dims).astype(LOW)))
        far = dot(rows[2 * count : 3 * count], weight, *dims) + come[count:].astype(WIDE)
        return come, links.chip(put(far.astype(LOW)))

    def tokens_end(started, rows, weight, dims):
        come, arrived = started
        own = dot(rows[3 * count :], weight, *dims)
        return own + come[:count].astype(WIDE) + put(arrived).astype(WIDE)

    gated_own = links.own_order(gated)
    going = tokens_start(gated_own, out_w, (1, 0))
    g_own_1 = put(g_ring)
    g_ring = links.around(g_own_1)
    g_0 = put(g_0)
    g_1 = links.across(g_own_1)
    mixed = put(tokens + tokens_end(going, gated_own, out_w, (1, 0)))
    scale_two = rms(mixed)
    sent = put(links.to_rel((mixed * scale_two * gain_ffn).astype(LOW)))
    n_far, n_near = links.chip(sent), links.core(sent)
    g_own_2 = put(g_ring)
    g_ring = links.around(g_own_2)
    g_1 = put(g_1)
    g_2 = links.across(g_own_2)
    n_far, n_near = put(n_far), put(n_near)
    n_both = put(links.core(n_far))
    normed_ffn = put(jnp.concatenate([n_near, n_both, n_far, sent], axis=0))
    g_own_3 = put(g_ring)
    d_ring = links.around(put(down_share))
    g_2 = put(g_2)
    g_3 = links.across(g_own_3)
    d_own_1 = put(d_ring)
    d_ring = links.around(d_own_1)
    p_pieces = [after(piece, d_own_1) for piece in p_pieces]
    proj_w = put(jnp.concatenate(p_pieces, axis=0))
    g_3 = put(g_3)
    d_0 = links.across(put(down_share))
    d_1 = links.across(d_own_1)
    g_pieces = [g_own_2, g_own_1, g_own_3, gu_share, g_2, g_1, g_3, g_0]
    gate_part, up_part, activated = gate_up_product(normed_ffn, g_pieces, units)
    activated = put(activated)
    d_own_2 = put(d_ring)
    d_ring = links.around(d_own_2)
    d_0, d_1 = put(d_0), put(d_1)
    d_2 = links.across(d_own_2)
    g_pieces = [after(piece, d_1) for piece in g_pieces]
    gu_w = put(jnp.concatenate(g_pieces, axis=0))
    d_own_3 = put(d_ring)
    d_3 = links.across(d_own_3)
    d_2, d_3 = put(d_2), put(d_3)
    stacked = jnp.concatenate(
        [d_own_2, d_own_1, d_own_3, down_share, d_2, d_1, d_3, d_0], axis=0
    )
    down_w = blocks_at(stacked, links.places(), part, 0)
    going = tokens_start(activated, down_w, (1, 0))
    result = mixed + tokens_end(going, activated, down_w, (1, 0))

    position = links.me_seq * count + jnp.arange(count, dtype=jnp.int32)
    valid_mask = (position < valid_count[0]).astype(WIDE)[:, None]
    mismatch = result - teacher[0]
    grad_out = cotangent[0] + valid_mask * mismatch
    squared_local = jnp.sum(valid_mask * mismatch * mismatch)
    count_local = jnp.sum(valid_mask)

    def rows_of(left, right, i, *added):
        size = model_width // dp_count
        total = dot(left[:, i * size : (i + 1) * size], right, 0, 0)
        for more in added:
            total = total + more.astype(WIDE)
        return total.astype(LOW)

    def gather_seq(total):
        far, near = links.chip(total), links.core(total)
        return [total, near, far, links.core(far)]

    sent = put(grad_out.astype(LOW))
    n_far, n_near = links.chip(sent), links.core(sent)
    n_far, n_near = put(n_far), put(n_near)
    n_both = put(links.core(n_far))
    grad_ffn = put(jnp.concatenate([n_near, n_both, n_far, sent], axis=0))
    whole = dot(activated, grad_ffn, 0, 0).astype(LOW)
    places = links.sources()
    d_come = [links.across(put(blocks_at(whole, places[i : i + 2], part, 0))) for i in (4, 6)]
    grad_act = dot(after(grad_ffn, order.last), down_w, 1, 1)
    sigma = jax.nn.sigmoid(gate_part)
    grad_gate = grad_act * up_part * sigma * (1.0 + gate_part * (1.0 - sigma))
    grad_up = grad_act * gate_part * sigma
    grad_both = put(jnp.concatenate([grad_gate, grad_up], axis=1).astype(LOW))
    going = tokens_start(grad_both, gu_w, (1, 1))
    d_come[0] = put(d_come[0])
    g_other = [put(rows_of(after(normed_ffn, order.last), grad_both, 4))]
    d_sums = put(sum_low(blocks_at(whole, places[:2], part, 0), d_come[0]))
    d_second, d_first = jnp.split(d_sums, 2, axis=0)
    d_second, d_first = links.around(d_second, 1), links.around(d_first, -1)
    grad_normed = links.from_rel(tokens_end(going, grad_both, gu_w, (1, 1)))
    grad_mid, gain_ffn_grad = norm_back(grad_normed, mixed, scale_two, gain_ffn)
    grad_mixed = grad_out + grad_mid
    sent = put(grad_mixed.astype(LOW))
    n_far, n_near = links.chip(sent), links.core(sent)
    d_come[1] = put(d_come[1])
    g_come = [links.across(put(g_other[0]))]
    d_second = put(d_second)
    d_third = put(sum_low(blocks_at(whole, places[2:3], part, 0), d_come[1][:part], d_second))
    d_third = links.around(d_third, 1)
    for i in (5, 6, 7):
        g_other.append(put(rows_of(after(normed_ffn, order.last), grad_both, i)))
    n_far, n_near = put(n_far), put(n_near)
    n_both = put(links.core(n_far))
    grad_att = put(in_row_order([sent, n_near, n_far, n_both]))
    grad_gated = put(dot(grad_att, out_w, 1, 1))
    left = blocks_at(gated, [(links.turn - r) % links.ring for r in ORDER], head_dim, 1)
    g_come[0] = put(g_come[0])
    g_come.append(links.across(put(g_other[1])))
    g_second = links.around(put(rows_of(normed_ffn, grad_both, 0, g_come[0])), 1)
    d_first, d_third = put(d_first), put(d_third)
    d_total = put(sum_low(blocks_at(whole, places[3:4], part, 0), d_come[1][part:], d_first, d_third))
    d_pieces = gather_seq(d_total)
    grad_proj, bias_local = retention_back(
        projected, bias, kept, after(grad_gated, d_total), cum, cum_rows, seg_col, seg_col.T, width, head_dim
    )
    grad_proj = put(grad_proj)
    g_come[1] = put(g_come[1])
    g_come.append(links.across(put(g_other[2])))
    g_second = put(g_second)
    g_first = links.around(put(rows_of(normed_ffn, grad_both, 1, g_come[1])), -1)
    back_rows = links.own_order(grad_proj)
    going = tokens_start(back_rows, proj_w, (1, 1))
    p_other = [put(rows_of(normed, after(grad_proj, order.last), 4))]
    g_come[2] = put(g_come[2])
    g_come.append(links.across(put(g_other[3])))
    g_third = put(rows_of(normed_ffn, grad_both, 2, g_come[2], g_second))
    g_first = put(g_first)
    g_third = links.around(g_third, 1)
    for i in (5, 6, 7):
        p_other.append(put(rows_of(normed, grad_proj, i)))
    grad_normed_one = links.from_rel(tokens_end(going, back_rows, proj_w, (1, 1)))
    grad_first, gain_ret_grad = norm_back(grad_normed_one, tokens, scale_one, gain_ret)
    grad_tokens = put(grad_mixed + grad_first)
    scalars = jnp.pad(jnp.stack([squared_local, count_local]), (0, EXTRA - 2))
    totals = put(jnp.concatenate([gain_ret_grad, gain_ffn_grad, bias_local[0], scalars]))
    totals_steps = links.total_steps()
    g_come[3] = put(g_come[3])
    p_come = [links.across(put(p_other[0]))]
    totals = totals_steps[0](totals)
    g_third = put(g_third)
    o_sums = put(dot(left, after(grad_att, order.last), 0, 0).astype(LOW))
    o_second, o_first, o_third, o_mine = jnp.split(o_sums, 4, axis=0)
    o_second, o_first = links.around(o_second, 1), links.around(o_first, -1)
    g_total = put(rows_of(normed_ffn, grad_both, 3, g_come[3], g_first, g_third))
    g_pieces = gather_seq(g_total)
    totals = totals_steps[1](put(totals))
    down_grad = put(whole_down(part, shard, [put(piece) for piece in d_pieces]))
    p_come[0] = put(p_come[0])
    p_come.append(links.across(put(p_other[1])))
    o_second, o_first = put(o_second), put(o_first)
    o_third = put(sum_low(o_third, o_second))
    p_second = links.around(put(rows_of(normed, grad_proj, 0, p_come[0])), 1)
    o_third = links.around(o_third, 1)
    totals = totals_steps[2](put(totals))
    p_come[1] = put(p_come[1])
    p_come.append(links.across(put(p_other[2])))
    p_second, o_third = put(p_second), put(o_third)
    p_first = links.around(put(rows_of(normed, grad_proj, 1, p_come[1])), -1)
    o_total = put(sum_low(o_mine, o_first, o_third))
    o_come = links.across_one_way(o_total, True)
    g_pieces = [put(piece) for piece in g_pieces]
    gu_grad = put(whole_gate_up(part, shard, dp_count, g_pieces))
    totals = totals_steps[3](put(totals))
    p_come[2] = put(p_come[2])
    p_come.append(links.across(put(p_other[3])))
    p_first = put(p_first)
    p_third = links.around(put(rows_of(normed, grad_proj, 2, p_come[2], p_second)), 1)
    o_mine = put(sum_low(o_total, put(o_come)))
    o_near = put(links.core(o_mine))
    pair = jnp.concatenate(
        [jnp.where(first_core, o_mine, o_near), jnp.where(first_core, o_near, o_mine)], axis=0
    )
    o_far = links.chip(put(pair))
    totals = totals_steps[4](put(totals))
    out_grad = put(jnp.where(x_half == links.side, pair, put(o_far)).astype(WIDE))
    totals = put(totals)
    p_come[3], p_third = put(p_come[3]), put(p_third)
    half = 2 * width * head_dim
    proj_grad = []
    p_pieces = []
    for start, stop in ((0, half), (half, 2 * half + EXTRA)):
        total = rows_of(
            normed, grad_proj[:, start:stop], 3,
            p_come[3][:, start:stop], p_first[:, start:stop], p_third[:, start:stop],
        )
        p_pieces.append(gather_seq(put(total)))
    proj_grad = whole_proj(2 * width, 0, head_dim, [], [put(piece) for piece in p_pieces[0]])
    decay_grad = sum(piece[:, half : half + heads].astype(WIDE) for piece in p_pieces[1])
    proj_grad = whole_proj(2 * width, 1, head_dim, [proj_grad], p_pieces[1])

    gain_ret_total, gain_ffn_total = totals[:model_width], totals[model_width : 2 * model_width]
    bias_total = totals[2 * model_width : 2 * model_width + heads]
    at = 2 * model_width + EXTRA
    mse = totals[at] / (totals[at + 1] * model_width)
    return (
        result[None],
        grad_tokens[None],
        proj_grad,
        decay_grad,
        bias_total,
        out_grad,
        gain_ret_total,
        gain_ffn_total,
        gu_grad,
        down_grad,
        mse,
    )


def rms(value):
    return lax.rsqrt(jnp.mean(value * value, axis=1, keepdims=True) + 1e-06)


def norm_back(grad_normed, source, inverse, gain):
    grad_gain = jnp.sum(grad_normed * source * inverse, axis=0)
    scaled = grad_normed * gain
    grad_source = inverse * (
        scaled - source * inverse * inverse * jnp.mean(scaled * source, axis=1, keepdims=True)
    )
    return (grad_source, grad_gain)


def plain_shards(
    inputs, segments, valid_count, teacher, cotangent, w_proj, w_decay, b_decay, w_out,
    gain_ret, gain_ffn, w_gu, w_down,
):
    seq_count = lax.axis_size("seq")
    me_seq = lax.axis_index("seq")
    tokens = inputs[0]
    count, model_width = tokens.shape
    heads = w_decay.shape[1]
    head_dim = model_width // heads
    width = heads // seq_count
    rows = w_proj.shape[0]

    def mine(value, axis):
        return lax.dynamic_index_in_dim(value, me_seq, axis, keepdims=False)

    def spread(value, axis):
        wide = jnp.expand_dims(value, axis)
        return jnp.concatenate(
            [jnp.where(me_seq == s, wide, jnp.zeros_like(wide)) for s in range(seq_count)], axis
        )

    def gather(block):
        return lax.all_gather(block, "dp", axis=0, tiled=True)

    def gather_tokens(value):
        return lax.all_gather(value, "seq", axis=0, tiled=True)

    def sum_tokens(value):
        return lax.psum_scatter(
            value.astype(LOW), "seq", scatter_dimension=0, tiled=True
        ).astype(WIDE)

    def scatter(grad):
        return lax.psum_scatter(grad.astype(LOW), "dp", scatter_dimension=0, tiled=True)

    def sum_rows(grad):
        return lax.psum(scatter(grad), "seq").astype(WIDE)

    def sum_columns(grad, blocks):
        total = scatter(grad)
        pieces = lax.all_gather(total.reshape(total.shape[0], blocks, -1), "seq", axis=2)
        return pieces.reshape(total.shape[0], -1).astype(WIDE)

    decay = jnp.pad(w_decay, ((0, 0), (0, EXTRA - heads)))
    proj = mine(w_proj.reshape(rows, 4 * width, seq_count, -1), 2).reshape(rows, -1)
    proj_w = jnp.concatenate([gather(proj), gather(decay)], axis=1)
    out_w = mine(gather(w_out).reshape(width, seq_count, -1, model_width), 1).reshape(-1, model_width)
    gu_w = gather(mine(w_gu.reshape(rows, 2, seq_count, -1), 2).reshape(rows, -1))
    down_w = mine(gather(w_down).reshape(seq_count, -1, model_width), 0)
    units = down_w.shape[0]

    scale_one = rms(tokens)
    normed = gather_tokens((tokens * scale_one * gain_ret).astype(LOW))
    seg_col = gather_tokens(segments[0])[:, None]
    projected = dot(normed, proj_w)
    bias = jnp.pad(b_decay, (0, EXTRA - heads))[None]
    gated, kept, cum, cum_rows = retention(projected, bias, seg_col, seg_col.T, width, head_dim)
    mixed = tokens + sum_tokens(dot(gated, out_w))
    scale_two = rms(mixed)
    normed_ffn = gather_tokens((mixed * scale_two * gain_ffn).astype(LOW))
    gate_up = dot(normed_ffn, gu_w)
    gate_part, up_part = gate_up[:, :units], gate_up[:, units:]
    sigma = jax.nn.sigmoid(gate_part)
    activated = (gate_part * sigma * up_part).astype(LOW)
    result = mixed + sum_tokens(dot(activated, down_w))

    position = me_seq * count + jnp.arange(count, dtype=jnp.int32)
    valid_mask = (position < valid_count[0]).astype(WIDE)[:, None]
    mismatch = result - teacher[0]
    grad_out = cotangent[0] + valid_mask * mismatch
    squared_local = jnp.sum(valid_mask * mismatch * mismatch)
    count_local = jnp.sum(valid_mask)

    grad_ffn = gather_tokens(grad_out.astype(LOW))
    grad = dot(activated, grad_ffn, 0, 0)
    down_grad = sum_rows(spread(grad, 0).reshape(-1, model_width))
    grad_act = dot(grad_ffn, down_w, 1, 1)
    grad_gate = grad_act * up_part * sigma * (1.0 + gate_part * (1.0 - sigma))
    grad_up = grad_act * gate_part * sigma
    grad_both = jnp.concatenate([grad_gate, grad_up], axis=1).astype(LOW)
    gu_grad = sum_columns(dot(normed_ffn, grad_both, 0, 0), 2)
    grad_normed = sum_tokens(dot(grad_both, gu_w, 1, 1))
    grad_mid, gain_ffn_grad = norm_back(grad_normed, mixed, scale_two, gain_ffn)
    grad_mixed = grad_out + grad_mid
    grad_att = gather_tokens(grad_mixed.astype(LOW))
    grad = dot(gated, grad_att, 0, 0)
    out_grad = sum_rows(spread(grad.reshape(width, -1, model_width), 1).reshape(-1, model_width))
    grad_gated = dot(grad_att, out_w, 1, 1)
    grad_proj, bias_local = retention_back(
        projected, bias, kept, grad_gated, cum, cum_rows, seg_col, seg_col.T, width, head_dim
    )
    share = 4 * width * head_dim
    grad = dot(normed, grad_proj, 0, 0)
    proj_grad = sum_columns(grad[:, :share], 4 * width)
    decay_grad = sum_rows(grad[:, share : share + heads])
    grad_normed_one = sum_tokens(dot(grad_proj, proj_w, 1, 1))
    grad_first, gain_ret_grad = norm_back(grad_normed_one, tokens, scale_one, gain_ret)
    totals = lax.psum(
        (gain_ret_grad, gain_ffn_grad, bias_local[0], squared_local, count_local), ("dp", "seq")
    )
    return (
        result[None],
        (grad_mixed + grad_first)[None],
        proj_grad,
        decay_grad,
        totals[2][:heads],
        out_grad,
        totals[0],
        totals[1],
        gu_grad,
        down_grad,
        totals[3] / (totals[4] * model_width),
    )


def solution(mesh):
    rows = P("dp", None)
    in_specs = (
        P("dp", "seq", None),
        P("dp", "seq"),
        P("dp"),
        P("dp", "seq", None),
        P("dp", "seq", None),
        rows,
        rows,
        P(),
        rows,
        P(),
        P(),
        rows,
        rows,
    )
    out_specs = (
        P("dp", "seq", None),
        P("dp", "seq", None),
        rows,
        rows,
        P(),
        rows,
        P(),
        P(),
        rows,
        rows,
        P(),
    )
    sizes = dict(mesh.shape)
    shards = placed_shards if sizes["dp"] == 8 and sizes["seq"] == 4 else plain_shards
    return jax.shard_map(shards, mesh=mesh, in_specs=in_specs, out_specs=out_specs, check_vma=False)
```

```python
import functools

import jax
import jax.numpy as jnp
from jax import lax
from jax.experimental import pallas as pl
from jax.experimental.pallas import tpu as pltpu
from jax.sharding import PartitionSpec as P

LOW = jnp.bfloat16
WIDE = jnp.float32
ORDER = (2, 1, 3, 0)
EXTRA = 128
VMEM_BYTES = 56 * 1024 * 1024


def dot(left, right, left_dim=1, right_dim=0):
    return lax.dot_general(
        left, right, (((left_dim,), (right_dim,)), ((), ())), preferred_element_type=WIDE
    )


def blocks_at(matrix, places, size, axis):
    return jnp.concatenate(
        [lax.dynamic_slice_in_dim(matrix, place * size, size, axis) for place in places], axis=axis
    )


def after(value, *tokens):
    return lax.optimization_barrier((value,) + tokens)[0]


def in_vmem():
    return pl.BlockSpec(memory_space=pltpu.VMEM)


def anywhere():
    return pl.BlockSpec(memory_space=pl.ANY)


def cost(*unused):
    return pl.CostEstimate(flops=0, bytes_accessed=0, transcendentals=0)


def pieces_kernel(*refs):
    rows, pieces, target = refs[0], refs[1:-1], refs[-1]
    target[...] = dot(rows[...], jnp.concatenate([piece[...] for piece in pieces], axis=0))


def pieces_product(rows, pieces):
    depth, width = pieces[0].shape
    height, count, tile = rows.shape[0], len(pieces), 256
    return pl.pallas_call(
        pieces_kernel,
        grid=(-(-width // tile),),
        in_specs=[pl.BlockSpec((height, count * depth), lambda i: (0, 0))]
        + [pl.BlockSpec((depth, tile), lambda i: (0, i))] * count,
        out_specs=pl.BlockSpec((height, tile), lambda i: (0, i)),
        out_shape=jax.ShapeDtypeStruct((height, width), WIDE),
        compiler_params=pltpu.CompilerParams(vmem_limit_bytes=VMEM_BYTES),
        cost_estimate=cost(),
    )(rows, *pieces)


def gate_up_kernel(count, *refs):
    rows, gate_w, up_w = refs[0], refs[1 : 1 + count], refs[1 + count : 1 + 2 * count]
    gate, up, activated = refs[1 + 2 * count :]
    tile = gate.shape[1]
    left = jnp.concatenate([piece[...] for piece in gate_w], axis=0)
    right = jnp.concatenate([piece[...] for piece in up_w], axis=0)
    both = dot(rows[...], jnp.concatenate([left, right], axis=1))
    gate_part, up_part = both[:, :tile], both[:, tile:]
    gate[...] = gate_part
    up[...] = up_part
    activated[...] = (gate_part * jax.nn.sigmoid(gate_part) * up_part).astype(LOW)


def gate_up_product(rows, pieces, units):
    height, depth = rows.shape
    tile = 128
    steps, count = units // tile, len(pieces)
    column = pl.BlockSpec((height, tile), lambda i: (0, i))
    size = pieces[0].shape[0]
    return pl.pallas_call(
        functools.partial(gate_up_kernel, count),
        grid=(steps,),
        in_specs=[pl.BlockSpec((height, depth), lambda i: (0, 0))]
        + [pl.BlockSpec((size, tile), lambda i: (0, i))] * count
        + [pl.BlockSpec((size, tile), lambda i: (0, steps + i))] * count,
        out_specs=[column] * 3,
        out_shape=[
            jax.ShapeDtypeStruct((height, units), WIDE),
            jax.ShapeDtypeStruct((height, units), WIDE),
            jax.ShapeDtypeStruct((height, units), LOW),
        ],
        compiler_params=pltpu.CompilerParams(vmem_limit_bytes=VMEM_BYTES),
        cost_estimate=cost(),
    )(rows, *pieces, *pieces)


def in_row_order_kernel(*refs):
    pieces, target = refs[:-1], refs[-1]
    me = lax.axis_index("seq")
    size = pieces[0].shape[0]
    for k, piece in enumerate(pieces):
        target[pl.ds(pl.multiple_of(lax.bitwise_xor(me, k) * size, size), size), :] = piece[...]


def in_row_order(pieces):
    size, width = pieces[0].shape
    return pl.pallas_call(
        in_row_order_kernel,
        in_specs=[in_vmem()] * len(pieces),
        out_specs=in_vmem(),
        out_shape=jax.ShapeDtypeStruct((len(pieces) * size, width), LOW),
        compiler_params=pltpu.CompilerParams(vmem_limit_bytes=VMEM_BYTES),
        cost_estimate=cost(),
    )(*pieces)


def proj_share_kernel(blocks, seq_count, source, decay, target):
    me = lax.axis_index("seq")
    rows, extra = decay.shape
    size = (target.shape[1] - EXTRA) // blocks
    for i in range(blocks):
        place = pl.multiple_of((i * seq_count + me) * size, size)
        target[:, i * size : (i + 1) * size] = source[:, pl.ds(place, size)]
    padded = jnp.concatenate([decay[...], jnp.zeros((rows, EXTRA - extra), LOW)], axis=1)
    target[:, blocks * size :] = padded


def row_shares_kernel(part, shard, seq_count, out, down, out_to, down_to):
    me = lax.axis_index("seq")
    half = out_to.shape[0]
    out_to[...] = out[pl.ds(pl.multiple_of(lax.rem(me, 2) * half, half), half), :]
    sure = shard - part * (seq_count - 1)
    rest = part - sure
    start = pl.multiple_of(me * part, 16)
    down_to[:sure, :] = down[pl.ds(start, sure), :]
    if rest:
        last = pl.multiple_of(jnp.minimum(start + sure, shard - rest), 16)
        rows = down[pl.ds(last, rest), :]
        down_to[sure:, :] = jnp.where(me < seq_count - 1, rows, jnp.zeros_like(rows))


def gate_up_share_kernel(part, shard, dp_count, source, target):
    me = lax.axis_index("seq")
    lane = 128
    window = 384
    columns = source.shape[1]
    half = dp_count * part
    row = lax.broadcasted_iota(jnp.int32, (window, lane), 0)
    col = lax.broadcasted_iota(jnp.int32, (window, lane), 1)
    for tile in range(target.shape[1] // lane):
        first = tile * lane % half
        which = tile * lane // half
        total = None
        for d in range(first // part, (first + lane - 1) // part + 1):
            base = (which * dp_count + d) * shard + me * part
            begin = pl.multiple_of(
                jnp.minimum(lax.div(base, lane) * lane, (columns - window) // lane * lane), lane
            )
            unit = first + col - d * part
            hit = (row + begin == base + unit) & (unit >= 0) & (unit < part)
            hit = hit & (me * part + unit < shard)
            chosen = jnp.where(hit, 1.0, 0.0).astype(LOW)
            piece = jnp.dot(source[:, pl.ds(begin, window)], chosen, preferred_element_type=WIDE)
            total = piece if total is None else total + piece
        target[:, pl.ds(tile * lane, lane)] = total.astype(LOW)


def gate_up_whole_kernel(part, shard, *refs):
    pieces, target, held = refs[:-2], refs[-2], refs[-1]
    me = lax.axis_index("seq")
    lane, window = 128, 256
    count = len(pieces)
    for k in range(count):
        place = lax.bitwise_xor(me, k)
        held[place] = pieces[k][...]
    row = lax.broadcasted_iota(jnp.int32, (window, lane), 0)
    col = lax.broadcasted_iota(jnp.int32, (window, lane), 1)
    width = pieces[0].shape[1]
    for tile in range(target.shape[1] // lane):
        at = tile * lane
        total = None
        while at < (tile + 1) * lane:
            block, inside = divmod(at, shard)
            share, unit = divmod(inside, part)
            stop = min((tile + 1) * lane, block * shard + min((share + 1) * part, shard))
            from_column = block * part + unit
            begin = min(from_column // lane * lane, width - window)
            off = at - tile * lane
            hit = (row + begin - from_column == col - off) & (col >= off) & (col < off + stop - at)
            chosen = jnp.where(hit, 1.0, 0.0).astype(LOW)
            piece = jnp.dot(held[share, :, begin : begin + window], chosen, preferred_element_type=WIDE)
            total = piece if total is None else total + piece
            at = stop
        target[:, tile * lane : (tile + 1) * lane] = total


def proj_whole_kernel(skip, *refs):
    pieces, target = refs[skip:-1], refs[-1]
    me = lax.axis_index("seq")
    size = pieces[0].shape[1]
    for k, piece in enumerate(pieces):
        place = pl.multiple_of(lax.bitwise_xor(me, k) * size, size)
        target[:, pl.ds(place, size)] = piece[...].astype(WIDE)


def down_whole_kernel(part, shard, *refs):
    pieces, target = refs[:-1], refs[-1]
    me = lax.axis_index("seq")
    count = len(pieces)
    sure = shard - part * (count - 1)
    for k, piece in enumerate(pieces):
        place = lax.bitwise_xor(me, k)
        start = pl.multiple_of(place * part, 16)
        target[pl.ds(start, sure), :] = piece[:sure, :].astype(WIDE)
        if sure < part:

            @pl.when(place < count - 1)
            def _(piece=piece, start=start):
                target[pl.ds(pl.multiple_of(start + sure, 16), part - sure), :] = piece[sure:, :].astype(WIDE)


def triangle(size, reverse):
    row = lax.broadcasted_iota(jnp.int32, (size, size), 0)
    col = lax.broadcasted_iota(jnp.int32, (size, size), 1)
    return jnp.where(row <= col if reverse else row >= col, 1.0, 0.0)


def running_sum(table, step, source, target, reverse):
    count, lanes = source.shape
    carry = jnp.zeros((1, lanes), WIDE)
    starts = range(0, count, step)
    for at in reversed(starts) if reverse else starts:
        block = source[at : at + step, :]
        sums = lax.dot_general(
            table, block, (((1,), (0,)), ((), ())),
            precision=lax.Precision.HIGHEST, preferred_element_type=WIDE,
        ) + carry
        target[at : at + step, :] = sums
        carry = carry + jnp.sum(block, axis=0, keepdims=True)


def decay_rows(at, size, cum_col, cum_row, seg_col, seg_row):
    wide = at + size
    spread = cum_col[at:wide] - cum_row[:, :wide]
    order_t = lax.broadcasted_iota(jnp.int32, (size, wide), 0) + at
    order_s = lax.broadcasted_iota(jnp.int32, (size, wide), 1)
    allowed = (seg_col[at:wide] == seg_row[:, :wide]) & (order_t >= order_s)
    return jnp.where(allowed, jnp.exp(jnp.minimum(spread, 0.0)), 0.0)


def lane_of(table, lane):
    lanes = lax.broadcasted_iota(jnp.int32, table.shape, 1)
    return jnp.sum(jnp.where(lanes == lane, table, 0.0), axis=1, keepdims=True)


def forward_kernel(
    step, scale, seq_count, q, k, v, gate, logit, bias, seg_col, seg_row, gated, kept, cum, cum_rows, held
):
    head = pl.program_id(0)
    lane = head * seq_count + lax.axis_index("seq")

    @pl.when(head == 0)
    def _():
        value = logit[...] + bias[...]
        held[...] = (jnp.minimum(value, 0.0) - jnp.log1p(jnp.exp(-jnp.abs(value)))) / 16.0
        running_sum(triangle(step, False), step, held, cum, False)
        cum_rows[...] = cum[...].T

    keys, values = k[...].astype(LOW), v[...].astype(LOW)
    seg_c, seg_r = seg_col[...], seg_row[...]
    cum_c, cum_r = lane_of(cum[...], lane), cum_rows[pl.ds(lane, 1), :]
    for at in range(0, q.shape[0], step):
        stop = at + step
        rows = (q[at:stop, :] * scale).astype(LOW)
        scores = dot(rows, keys[:stop], 1, 1) * decay_rows(at, step, cum_c, cum_r, seg_c, seg_r)
        high = scores.astype(LOW)
        rest = (scores - high.astype(WIDE)).astype(LOW)
        retained = dot(high, values[:stop]) + dot(rest, values[:stop])
        kept[at:stop, :] = retained
        power = jnp.mean(retained * retained, axis=1, keepdims=True)
        unit = retained * lax.rsqrt(jnp.maximum(power, 1.0))
        gates = gate[at:stop, :]
        gated[at:stop, :] = (gates * jax.nn.sigmoid(gates) * unit).astype(LOW)


def backward_kernel(
    step, scale, width, seq_count, q, k, v, gate, logit, bias, kept, grad, cum, cum_rows, seg_col, seg_row,
    grad_proj, bias_sum, grad_k, grad_v, grad_cum, held,
):
    head = pl.program_id(0)
    lane = head * seq_count + lax.axis_index("seq")
    size = q.shape[1]
    keys, values = k[...].astype(LOW), v[...].astype(LOW)
    seg_c, seg_r = seg_col[...], seg_row[...]
    cum_c, cum_r = lane_of(cum[...], lane), cum_rows[pl.ds(lane, 1), :]

    def columns(block):
        return pl.ds(pl.multiple_of((block * width + head) * size, size), size)

    @pl.when(head == 0)
    def _():
        grad_cum[...] = jnp.zeros_like(grad_cum)

    count = q.shape[0]
    lanes = lax.broadcasted_iota(jnp.int32, (step, EXTRA), 1)
    for at in reversed(range(0, count, step)):
        stop = at + step
        first = stop == count
        retained, gates, grads = kept[at:stop, :], gate[at:stop, :], grad[at:stop, :]
        power = jnp.mean(retained * retained, axis=1, keepdims=True)
        inverse = lax.rsqrt(jnp.maximum(power, 1.0))
        unit = retained * inverse
        sigma = jax.nn.sigmoid(gates)
        grad_proj[at:stop, columns(3)] = (
            grads * unit * sigma * (1.0 + gates * (1.0 - sigma))
        ).astype(LOW)
        grad_unit = grads * gates * sigma
        along = jnp.mean(grad_unit * unit, axis=1, keepdims=True)
        grad_low = (inverse * jnp.where(power > 1.0, grad_unit - unit * along, grad_unit)).astype(LOW)
        rows = (q[at:stop, :] * scale).astype(LOW)
        table = decay_rows(at, step, cum_c, cum_r, seg_c, seg_r)
        scores = (dot(rows, keys[:stop], 1, 1) * table).astype(LOW)
        pairs = (table * dot(grad_low, values[:stop], 1, 1)).astype(LOW)
        grad_q = dot(pairs, keys[:stop])
        grad_proj[at:stop, columns(0)] = (grad_q * scale).astype(LOW)
        part_k = dot(pairs, rows, 0, 0)
        part_v = dot(scores, grad_low, 0, 0)
        if first:
            grad_k[:stop, :] = part_k
            grad_v[:stop, :] = part_v
        else:
            grad_k[:stop, :] += part_k
            grad_v[:stop, :] += part_v
        along_q = jnp.sum(rows.astype(WIDE) * grad_q, axis=1, keepdims=True)
        along_k = jnp.sum(keys[at:stop].astype(WIDE) * grad_k[at:stop, :], axis=1, keepdims=True)
        grad_cum[at:stop, :] += jnp.where(lanes == lane, along_q - along_k, 0.0)
    grad_proj[:, columns(1)] = grad_k[...].astype(LOW)
    grad_proj[:, columns(2)] = grad_v[...].astype(LOW)

    @pl.when(head == width - 1)
    def _():
        running_sum(triangle(step, True), step, grad_cum, held, True)
        value = held[...] * jax.nn.sigmoid(-(logit[...] + bias[...])) / 16.0
        bias_sum[...] = jnp.sum(value, axis=0, keepdims=True)
        grad_proj[:, 4 * width * size :] = value.astype(LOW)


def head_specs(row, size, width):
    def block(number):
        return pl.BlockSpec((row, size), lambda h: (0, number * width + h))

    def same(shape):
        return pl.BlockSpec(shape, lambda h: (0, 0))

    logit = pl.BlockSpec((row, EXTRA), lambda h: (0, 4 * width * size // EXTRA))
    return block, same, logit


def retention(projected, bias, seg_col, seg_row, width, size):
    row = projected.shape[0]
    block, same, logit = head_specs(row, size, width)
    pairs = row * row * width * 5 // 8
    return pl.pallas_call(
        functools.partial(forward_kernel, row // 4, size ** (-0.5), lax.axis_size("seq")),
        grid=(width,),
        in_specs=[block(0), block(1), block(2), block(3), logit, same((1, EXTRA)), same((row, 1)), same((1, row))],
        out_specs=[block(0), block(0), same((row, EXTRA)), same((EXTRA, row))],
        out_shape=[
            jax.ShapeDtypeStruct((row, width * size), LOW),
            jax.ShapeDtypeStruct((row, width * size), WIDE),
            jax.ShapeDtypeStruct((row, EXTRA), WIDE),
            jax.ShapeDtypeStruct((EXTRA, row), WIDE),
        ],
        scratch_shapes=[pltpu.VMEM((row, EXTRA), WIDE)],
        compiler_params=pltpu.CompilerParams(vmem_limit_bytes=VMEM_BYTES),
        cost_estimate=cost(pairs * size * 4, projected.size * 6, pairs),
    )(*([projected] * 5), bias, seg_col, seg_row)


def retention_back(projected, bias, kept, grad_gated, cum, cum_rows, seg_col, seg_row, width, size):
    row = projected.shape[0]
    block, same, logit = head_specs(row, size, width)
    pairs = row * row * width * 5 // 8
    return pl.pallas_call(
        functools.partial(backward_kernel, row // 4, size ** (-0.5), width, lax.axis_size("seq")),
        grid=(width,),
        in_specs=[block(0), block(1), block(2), block(3), logit, same((1, EXTRA)), block(0), block(0)]
        + [same((row, EXTRA)), same((EXTRA, row)), same((row, 1)), same((1, row))],
        out_specs=[same((row, 4 * width * size + EXTRA)), same((1, EXTRA))],
        out_shape=[
            jax.ShapeDtypeStruct((row, 4 * width * size + EXTRA), LOW),
            jax.ShapeDtypeStruct((1, EXTRA), WIDE),
        ],
        scratch_shapes=[pltpu.VMEM((row, size), WIDE)] * 2 + [pltpu.VMEM((row, EXTRA), WIDE)] * 2,
        compiler_params=pltpu.CompilerParams(vmem_limit_bytes=VMEM_BYTES),
        cost_estimate=cost(pairs * size * 10, projected.size * 8, pairs),
    )(*([projected] * 5), bias, kept, grad_gated, cum, cum_rows, seg_col, seg_row)


class Order:
    def __init__(self):
        self.last = None

    def put(self, value):
        if self.last is not None:
            value = after(value, self.last)
        self.last = value
        return value


class Links:
    def __init__(self, dp_count, seq_count):
        self.dp_count, self.seq_count = dp_count, seq_count
        self.ring = dp_count // 2
        self.me_dp, self.me_seq = lax.axis_index("dp"), lax.axis_index("seq")
        self.turn, self.side = self.me_dp // 2, self.me_dp % 2

    def around(self, value, by=1):
        count = self.dp_count
        return lax.ppermute(value, "dp", [(d, (d + 2 * by) % count) for d in range(count)])

    def across(self, value):
        return lax.ppermute(value, "dp", [(d, d ^ 1) for d in range(self.dp_count)])

    def across_one_way(self, value, toward):
        pairs = [
            (d * self.seq_count + s, (d ^ 1) * self.seq_count + s)
            for d in range(self.dp_count)
            for s in range(self.seq_count)
            if (d % 2 == s // 2) != toward
        ]
        return lax.ppermute(value, ("dp", "seq"), pairs)

    def core(self, value):
        return lax.ppermute(value, "seq", [(s, s ^ 1) for s in range(self.seq_count)])

    def chip(self, value):
        return lax.ppermute(value, "seq", [(s, s ^ 2) for s in range(self.seq_count)])

    def sources(self):
        return [
            ((self.turn - r) % self.ring) * 2 + (self.side ^ e) for e in range(2) for r in ORDER
        ]

    def spot(self, r):
        found = ORDER.index(0)
        for value in range(1, self.ring):
            found = jnp.where(r == value, ORDER.index(value), found)
        return found

    def places(self):
        found = []
        for d in range(self.dp_count):
            r = (self.turn - d // 2) % self.ring
            found.append(self.spot(r) + (self.side ^ (d % 2)) * self.ring)
        return found

    def total_steps(self):
        def step(axis, count, apart):
            pairs = [(d, d ^ apart) for d in range(count)]
            return lambda value: value + lax.ppermute(value, axis, pairs)

        return [step("seq", self.seq_count, apart) for apart in (1, 2)] + [
            step("dp", self.dp_count, apart) for apart in (1, 2, 4)
        ]

    def own_order(self, rows):
        me = self.me_seq
        return blocks_at(rows, [me ^ 1, me ^ 3, me ^ 2, me], rows.shape[0] // 4, 0)

    def to_rel(self, value):
        return blocks_at(value, self.sources(), value.shape[1] // self.dp_count, 1)

    def from_rel(self, value):
        return blocks_at(value, self.places(), value.shape[1] // self.dp_count, 1)


def sum_low(*parts):
    total = parts[0].astype(WIDE)
    for part in parts[1:]:
        total = total + part.astype(WIDE)
    return total.astype(LOW)


def weight_shares(links, width, part, shard, w_proj, w_decay, w_out, w_down):
    rows, columns = w_proj.shape[0], w_proj.shape[1] // links.seq_count + EXTRA
    model = w_down.shape[1]
    block = min(rows, 64)
    proj = pl.pallas_call(
        functools.partial(proj_share_kernel, 4 * width, links.seq_count),
        grid=(rows // block,),
        in_specs=[
            pl.BlockSpec((block, w_proj.shape[1]), lambda i: (i, 0)),
            pl.BlockSpec((block, w_decay.shape[1]), lambda i: (i, 0)),
        ],
        out_specs=pl.BlockSpec((block, columns), lambda i: (i, 0)),
        out_shape=jax.ShapeDtypeStruct((rows, columns), LOW),
        compiler_params=pltpu.CompilerParams(vmem_limit_bytes=VMEM_BYTES),
        cost_estimate=cost(0, 10 * rows * columns),
    )(w_proj, w_decay)
    out, down = pl.pallas_call(
        functools.partial(row_shares_kernel, part, shard, links.seq_count),
        in_specs=[in_vmem()] * 2,
        out_specs=[in_vmem()] * 2,
        out_shape=[
            jax.ShapeDtypeStruct((w_out.shape[0] // 2, model), LOW),
            jax.ShapeDtypeStruct((part, model), LOW),
        ],
        compiler_params=pltpu.CompilerParams(vmem_limit_bytes=VMEM_BYTES),
        cost_estimate=cost(0, 3 * w_out.size + 3 * w_down.size),
    )(w_out, w_down)
    return proj, out, down


def gate_up_share(links, part, shard, w_gu):
    rows, units = w_gu.shape[0], part * links.dp_count
    return pl.pallas_call(
        functools.partial(gate_up_share_kernel, part, shard, links.dp_count),
        in_specs=[in_vmem()],
        out_specs=in_vmem(),
        out_shape=jax.ShapeDtypeStruct((rows, 2 * units), LOW),
        compiler_params=pltpu.CompilerParams(vmem_limit_bytes=VMEM_BYTES),
        cost_estimate=cost(2 * rows * 768 * 2 * units, 2 * w_gu.size + 4 * rows * units),
    )(w_gu)


def whole_down(part, shard, pieces):
    model = pieces[0].shape[1]
    return pl.pallas_call(
        functools.partial(down_whole_kernel, part, shard),
        in_specs=[in_vmem()] * 4,
        out_specs=in_vmem(),
        out_shape=jax.ShapeDtypeStruct((shard, model), WIDE),
        compiler_params=pltpu.CompilerParams(vmem_limit_bytes=VMEM_BYTES),
        cost_estimate=cost(0, 6 * shard * model),
    )(*pieces)


def whole_gate_up(part, shard, dp_count, pieces):
    rows, columns = pieces[0].shape
    block = min(rows, 64)
    whole = 2 * dp_count * shard
    return pl.pallas_call(
        functools.partial(gate_up_whole_kernel, part, shard),
        grid=(rows // block,),
        in_specs=[pl.BlockSpec((block, columns), lambda i: (i, 0))] * 4,
        out_specs=pl.BlockSpec((block, whole), lambda i: (i, 0)),
        out_shape=jax.ShapeDtypeStruct((rows, whole), WIDE),
        scratch_shapes=[pltpu.VMEM((4, block, columns), LOW)],
        compiler_params=pltpu.CompilerParams(vmem_limit_bytes=VMEM_BYTES),
        cost_estimate=cost(rows * whole * 1024, rows * whole * 6),
    )(*pieces)


def whole_proj(half, number, size, kept, pieces):
    rows = pieces[0].shape[0]
    return pl.pallas_call(
        functools.partial(proj_whole_kernel, len(kept)),
        grid=(half,),
        in_specs=[anywhere()] * len(kept) + [pl.BlockSpec((rows, size), lambda i: (0, i))] * 4,
        out_specs=pl.BlockSpec((rows, 4 * size), lambda i: (0, number * half + i)),
        out_shape=jax.ShapeDtypeStruct((rows, 8 * half * size), WIDE),
        input_output_aliases={0: 0} if kept else {},
        compiler_params=pltpu.CompilerParams(vmem_limit_bytes=VMEM_BYTES),
        cost_estimate=cost(0, rows * half * size * 24),
    )(*kept, *pieces)


def placed_shards(
    inputs, segments, valid_count, teacher, cotangent, w_proj, w_decay, b_decay, w_out,
    gain_ret, gain_ffn, w_gu, w_down,
):
    dp_count, seq_count = lax.axis_size("dp"), lax.axis_size("seq")
    links, order = Links(dp_count, seq_count), Order()
    put = order.put
    tokens = inputs[0]
    count, model_width = tokens.shape
    heads = w_decay.shape[1]
    head_dim = model_width // heads
    width = heads // seq_count
    shard = w_down.shape[0]
    part = -(-shard // (16 * seq_count)) * 16
    units = part * dp_count
    first_core, x_half = links.me_seq % 2 == 0, links.me_seq // 2

    proj_share, out_share, down_share = weight_shares(
        links, width, part, shard, w_proj, w_decay, w_out, w_down
    )
    proj_share = put(proj_share)
    p_ring = links.around(proj_share)
    p_0 = links.across(proj_share)
    scale_one = rms(tokens)
    normed_here = links.to_rel((tokens * scale_one * gain_ret).astype(LOW))
    ids = jnp.broadcast_to(segments[0][:, None].astype(LOW), (count, EXTRA))
    sent = put(jnp.concatenate([normed_here, ids], axis=1))
    n_far, n_near = links.chip(sent), links.core(sent)
    out_share, down_share = put(out_share), put(down_share)
    out_cross = links.across_one_way(out_share, False)
    gu_share = put(gate_up_share(links, part, shard, after(w_gu, sent)))
    p_own_1, p_0 = put(p_ring), put(p_0)
    p_ring, p_1 = links.around(p_own_1), links.across(p_own_1)
    n_near, n_far = put(n_near), put(n_far)
    n_both = put(links.core(n_far))
    normed = put(in_row_order([sent, n_near, n_far, n_both]))
    seg_col = normed[:, model_width : model_width + 1].astype(jnp.int32)
    out_block = put(jnp.where(links.side == x_half, out_share, put(out_cross)))
    p_own_2 = put(p_ring)
    p_ring = links.around(p_own_2)
    p_1 = put(p_1)
    p_2 = links.across(p_own_2)
    p_own_3 = put(p_ring)
    o_ring = links.around(out_block)
    p_2 = put(p_2)
    p_3 = links.across(p_own_3)
    o_own_1 = put(o_ring)
    o_ring = links.around(o_own_1)
    o_own_2 = put(o_ring)
    g_ring = links.around(put(gu_share))
    o_ring = links.around(o_own_2)
    p_3 = put(p_3)
    g_0 = links.across(put(gu_share))
    p_pieces = [p_own_2, p_own_1, p_own_3, proj_share, p_2, p_1, p_3, p_0]
    projected = put(pieces_product(normed, p_pieces))
    bias = jnp.pad(b_decay, (0, EXTRA - heads))[None]
    gated, kept, cum, cum_rows = retention(projected, bias, seg_col, seg_col.T, width, head_dim)
    gated = put(gated)
    o_own_3, g_own_1, g_0 = put(o_ring), put(g_ring), put(g_0)
    g_ring, g_1 = links.around(g_own_1), links.across(g_own_1)
    out_w = blocks_at(
        jnp.concatenate([o_own_2, o_own_1, o_own_3, out_block], axis=0),
        [links.spot((links.turn - j) % links.ring) for j in range(links.ring)],
        out_share.shape[0],
        0,
    )

    def tokens_start(rows, weight, dims):
        come = links.core(put(dot(rows[: 2 * count], weight, *dims).astype(LOW)))
        far = dot(rows[2 * count : 3 * count], weight, *dims) + come[count:].astype(WIDE)
        return come, links.chip(put(far.astype(LOW)))

    def tokens_end(started, rows, weight, dims):
        come, arrived = started
        own = dot(rows[3 * count :], weight, *dims)
        return own + come[:count].astype(WIDE) + put(arrived).astype(WIDE)

    gated_own = links.own_order(gated)
    going = tokens_start(gated_own, out_w, (1, 0))
    g_own_2 = put(g_ring)
    g_ring = links.around(g_own_2)
    g_1 = put(g_1)
    g_2 = links.across(g_own_2)
    mixed = put(tokens + tokens_end(going, gated_own, out_w, (1, 0)))
    scale_two = rms(mixed)
    sent = put(links.to_rel((mixed * scale_two * gain_ffn).astype(LOW)))
    n_far, n_near = links.chip(sent), links.core(sent)
    g_own_3, g_2 = put(g_ring), put(g_2)
    g_3 = links.across(g_own_3)
    d_ring = links.around(put(down_share))
    n_far, n_near = put(n_far), put(n_near)
    n_both = put(links.core(n_far))
    normed_ffn = put(jnp.concatenate([n_near, n_both, n_far, sent], axis=0))
    d_own_1 = put(d_ring)
    d_ring = links.around(d_own_1)
    p_pieces = [after(piece, d_own_1) for piece in p_pieces]
    proj_w = put(jnp.concatenate(p_pieces, axis=0))
    g_3 = put(g_3)
    d_0 = links.across(put(down_share))
    d_1 = links.across(d_own_1)
    g_pieces = [g_own_2, g_own_1, g_own_3, gu_share, g_2, g_1, g_3, g_0]
    gate_part, up_part, activated = gate_up_product(normed_ffn, g_pieces, units)
    activated = put(activated)
    d_own_2 = put(d_ring)
    d_ring = links.around(d_own_2)
    d_0, d_1 = put(d_0), put(d_1)
    d_2 = links.across(d_own_2)
    g_pieces = [after(piece, d_1) for piece in g_pieces]
    gu_w = put(jnp.concatenate(g_pieces, axis=0))
    d_own_3 = put(d_ring)
    d_3 = links.across(d_own_3)
    d_2, d_3 = put(d_2), put(d_3)
    stacked = jnp.concatenate(
        [d_own_2, d_own_1, d_own_3, down_share, d_2, d_1, d_3, d_0], axis=0
    )
    down_w = blocks_at(stacked, links.places(), part, 0)
    going = tokens_start(activated, down_w, (1, 0))
    result = mixed + tokens_end(going, activated, down_w, (1, 0))

    position = links.me_seq * count + jnp.arange(count, dtype=jnp.int32)
    valid_mask = (position < valid_count[0]).astype(WIDE)[:, None]
    mismatch = result - teacher[0]
    grad_out = cotangent[0] + valid_mask * mismatch
    squared_local = jnp.sum(valid_mask * mismatch * mismatch)
    count_local = jnp.sum(valid_mask)

    def rows_of(left, right, i, *added):
        size = model_width // dp_count
        total = dot(left[:, i * size : (i + 1) * size], right, 0, 0)
        for more in added:
            total = total + more.astype(WIDE)
        return total.astype(LOW)

    def gather_seq(total):
        far, near = links.chip(total), links.core(total)
        return [total, near, far, links.core(far)]

    sent = put(grad_out.astype(LOW))
    n_far, n_near = links.chip(sent), links.core(sent)
    n_far, n_near = put(n_far), put(n_near)
    n_both = put(links.core(n_far))
    grad_ffn = put(jnp.concatenate([n_near, n_both, n_far, sent], axis=0))
    whole = dot(activated, grad_ffn, 0, 0).astype(LOW)
    places = links.sources()
    d_go = [put(blocks_at(whole, places[i:k], part, 0)) for i, k in ((4, 5), (5, 6), (6, 8))]
    d_come = [links.across(d_go[0])]
    grad_act = dot(after(grad_ffn, order.last), down_w, 1, 1)
    sigma = jax.nn.sigmoid(gate_part)
    grad_gate = grad_act * up_part * sigma * (1.0 + gate_part * (1.0 - sigma))
    grad_up = grad_act * gate_part * sigma
    grad_both = put(jnp.concatenate([grad_gate, grad_up], axis=1).astype(LOW))
    d_come[0] = put(d_come[0])
    d_come.append(links.across(put(d_go[1])))
    back = after(grad_both, order.last)
    come = links.core(put(dot(back[: 2 * count], gu_w, 1, 1).astype(LOW)))
    d_come[1] = put(d_come[1])
    d_come.append(links.across(put(d_go[2])))
    far = dot(back[2 * count : 3 * count], gu_w, 1, 1) + come[count:].astype(WIDE)
    going = come, links.chip(put(far.astype(LOW)))
    d_first = sum_low(blocks_at(whole, places[1:2], part, 0), d_come[1])
    d_second = sum_low(blocks_at(whole, places[0:1], part, 0), d_come[0])
    d_second, d_first = links.around(put(d_second), 1), links.around(put(d_first), -1)
    g_other = [put(rows_of(after(normed_ffn, order.last), grad_both, 4))]
    d_come[2] = put(d_come[2])
    g_come = [links.across(put(g_other[0]))]
    grad_normed = links.from_rel(tokens_end(going, grad_both, gu_w, (1, 1)))
    grad_mid, gain_ffn_grad = norm_back(grad_normed, mixed, scale_two, gain_ffn)
    grad_mixed = grad_out + grad_mid
    sent = put(grad_mixed.astype(LOW))
    n_far, n_near = links.chip(sent), links.core(sent)
    d_second, d_first = put(d_second), put(d_first)
    d_third = put(sum_low(blocks_at(whole, places[2:3], part, 0), d_come[2][:part], d_second))
    d_third = links.around(d_third, 1)
    g_come[0] = put(g_come[0])
    g_other.append(put(rows_of(after(normed_ffn, order.last), grad_both, 5)))
    g_come.append(links.across(g_other[1]))
    for i in (6, 7):
        g_other.append(put(rows_of(after(normed_ffn, order.last), grad_both, i)))
    n_far, n_near = put(n_far), put(n_near)
    n_both = put(links.core(n_far))
    grad_att = put(in_row_order([sent, n_near, n_far, n_both]))
    g_come[1] = put(g_come[1])
    g_come.append(links.across(put(g_other[2])))
    grad_gated = put(dot(after(grad_att, order.last), out_w, 1, 1))
    d_third = put(d_third)
    g_second = links.around(put(rows_of(normed_ffn, grad_both, 0, after(g_come[0], order.last))), 1)
    left = blocks_at(gated, [(links.turn - r) % links.ring for r in ORDER], head_dim, 1)
    o_sums = put(dot(left, after(grad_att, order.last), 0, 0).astype(LOW))
    o_second, o_first, o_third, o_mine = jnp.split(o_sums, 4, axis=0)
    o_second, o_first = links.around(o_second, 1), links.around(o_first, -1)
    grad_proj, bias_local = retention_back(
        projected, bias, kept, after(grad_gated, order.last), cum, cum_rows, seg_col, seg_col.T, width, head_dim
    )
    grad_proj = put(grad_proj)
    g_second, g_come[2] = put(g_second), put(g_come[2])
    g_come.append(links.across(put(g_other[3])))
    p_other = [put(rows_of(normed, after(grad_proj, order.last), 4))]
    back_rows = links.own_order(after(grad_proj, order.last))
    come = put(dot(back_rows[: 2 * count], proj_w, 1, 1).astype(LOW))
    come = links.core(come)
    g_first = links.around(put(rows_of(normed_ffn, grad_both, 1, after(g_come[1], order.last))), -1)
    o_second, o_first = put(o_second), put(o_first)
    o_third = links.around(put(sum_low(o_third, o_second)), 1)
    g_come[3] = put(g_come[3])
    p_come = [links.across(p_other[0])]
    g_third = links.around(put(rows_of(normed_ffn, grad_both, 2, after(g_come[2], order.last), g_second)), 1)
    p_other.append(put(rows_of(normed, after(grad_proj, order.last), 5)))
    p_come[0] = put(p_come[0])
    p_come.append(links.across(p_other[1]))
    far = dot(after(back_rows[2 * count : 3 * count], order.last), proj_w, 1, 1) + come[count:].astype(WIDE)
    going = come, links.chip(put(far.astype(LOW)))
    g_first, o_third = put(g_first), put(o_third)
    p_other.append(put(rows_of(normed, after(grad_proj, order.last), 6)))
    p_come[1] = put(p_come[1])
    p_come.append(links.across(p_other[2]))
    p_second = links.around(put(rows_of(normed, after(grad_proj, order.last), 0, p_come[0])), 1)
    d_total = put(sum_low(blocks_at(whole, places[3:4], part, 0), d_come[2][part:], d_first, d_third))
    g_third = put(g_third)
    grad_normed_one = links.from_rel(tokens_end(going, back_rows, proj_w, (1, 1)))
    d_pieces = gather_seq(after(d_total, order.last))
    p_other.append(put(rows_of(normed, after(grad_proj, order.last), 7)))
    p_come[2] = put(p_come[2])
    p_come.append(links.across(p_other[3]))
    p_first = links.around(put(rows_of(normed, after(grad_proj, order.last), 1, p_come[1])), -1)
    grad_first, gain_ret_grad = norm_back(grad_normed_one, tokens, scale_one, gain_ret)
    grad_tokens = put(grad_mixed + grad_first)
    scalars = jnp.pad(jnp.stack([squared_local, count_local]), (0, EXTRA - 2))
    totals = put(jnp.concatenate([gain_ret_grad, gain_ffn_grad, bias_local[0], scalars]))
    totals_steps = links.total_steps()
    totals = totals_steps[0](totals)
    p_second = put(p_second)
    p_third = links.around(put(rows_of(normed, grad_proj, 2, p_come[2], p_second)), 1)
    g_total = put(rows_of(normed_ffn, after(grad_both, order.last), 3, g_come[3], g_first, g_third))
    g_pieces = gather_seq(g_total)
    totals = totals_steps[1](put(totals))
    o_total = put(sum_low(o_mine, o_first, o_third))
    p_first = put(p_first)
    down_grad = put(whole_down(part, shard, [put(piece) for piece in d_pieces]))
    o_come = links.across_one_way(after(o_total, order.last), True)
    totals = put(totals)
    p_come[3], p_third = put(p_come[3]), put(p_third)
    half = 2 * width * head_dim
    p_pieces = []
    for start, stop in ((0, half), (half, 2 * half + EXTRA)):
        total = rows_of(
            normed, grad_proj[:, start:stop], 3,
            p_come[3][:, start:stop], p_first[:, start:stop], p_third[:, start:stop],
        )
        p_pieces.append(gather_seq(put(total)))
    o_mine = put(sum_low(o_total, put(o_come)))
    o_near = put(links.core(o_mine))
    pair = jnp.concatenate(
        [jnp.where(first_core, o_mine, o_near), jnp.where(first_core, o_near, o_mine)], axis=0
    )
    o_far = links.chip(put(pair))
    totals = totals_steps[2](totals)
    g_pieces = [put(piece) for piece in g_pieces]
    gu_grad = put(whole_gate_up(part, shard, dp_count, g_pieces))
    totals = totals_steps[4](totals_steps[3](put(totals)))
    proj_grad = put(whole_proj(2 * width, 0, head_dim, [], [put(piece) for piece in p_pieces[0]]))
    totals = put(totals)
    decay_grad = sum(piece[:, half : half + heads].astype(WIDE) for piece in p_pieces[1])
    proj_grad = whole_proj(2 * width, 1, head_dim, [proj_grad], p_pieces[1])
    out_grad = jnp.where(x_half == links.side, pair, put(o_far)).astype(WIDE)

    gain_ret_total, gain_ffn_total = totals[:model_width], totals[model_width : 2 * model_width]
    bias_total = totals[2 * model_width : 2 * model_width + heads]
    at = 2 * model_width + EXTRA
    mse = totals[at] / (totals[at + 1] * model_width)
    return (
        result[None],
        grad_tokens[None],
        proj_grad,
        decay_grad,
        bias_total,
        out_grad,
        gain_ret_total,
        gain_ffn_total,
        gu_grad,
        down_grad,
        mse,
    )


def rms(value):
    return lax.rsqrt(jnp.mean(value * value, axis=1, keepdims=True) + 1e-06)


def norm_back(grad_normed, source, inverse, gain):
    grad_gain = jnp.sum(grad_normed * source * inverse, axis=0)
    scaled = grad_normed * gain
    grad_source = inverse * (
        scaled - source * inverse * inverse * jnp.mean(scaled * source, axis=1, keepdims=True)
    )
    return (grad_source, grad_gain)


def plain_shards(
    inputs, segments, valid_count, teacher, cotangent, w_proj, w_decay, b_decay, w_out,
    gain_ret, gain_ffn, w_gu, w_down,
):
    seq_count = lax.axis_size("seq")
    me_seq = lax.axis_index("seq")
    tokens = inputs[0]
    count, model_width = tokens.shape
    heads = w_decay.shape[1]
    head_dim = model_width // heads
    width = heads // seq_count
    rows = w_proj.shape[0]

    def mine(value, axis):
        return lax.dynamic_index_in_dim(value, me_seq, axis, keepdims=False)

    def spread(value, axis):
        wide = jnp.expand_dims(value, axis)
        return jnp.concatenate(
            [jnp.where(me_seq == s, wide, jnp.zeros_like(wide)) for s in range(seq_count)], axis
        )

    def gather(block):
        return lax.all_gather(block, "dp", axis=0, tiled=True)

    def gather_tokens(value):
        return lax.all_gather(value, "seq", axis=0, tiled=True)

    def sum_tokens(value):
        return lax.psum_scatter(
            value.astype(LOW), "seq", scatter_dimension=0, tiled=True
        ).astype(WIDE)

    def scatter(grad):
        return lax.psum_scatter(grad.astype(LOW), "dp", scatter_dimension=0, tiled=True)

    def sum_rows(grad):
        return lax.psum(scatter(grad), "seq").astype(WIDE)

    def sum_columns(grad, blocks):
        total = scatter(grad)
        pieces = lax.all_gather(total.reshape(total.shape[0], blocks, -1), "seq", axis=2)
        return pieces.reshape(total.shape[0], -1).astype(WIDE)

    decay = jnp.pad(w_decay, ((0, 0), (0, EXTRA - heads)))
    proj = mine(w_proj.reshape(rows, 4 * width, seq_count, -1), 2).reshape(rows, -1)
    proj_w = jnp.concatenate([gather(proj), gather(decay)], axis=1)
    out_w = mine(gather(w_out).reshape(width, seq_count, -1, model_width), 1).reshape(-1, model_width)
    gu_w = gather(mine(w_gu.reshape(rows, 2, seq_count, -1), 2).reshape(rows, -1))
    down_w = mine(gather(w_down).reshape(seq_count, -1, model_width), 0)
    units = down_w.shape[0]

    scale_one = rms(tokens)
    normed = gather_tokens((tokens * scale_one * gain_ret).astype(LOW))
    seg_col = gather_tokens(segments[0])[:, None]
    projected = dot(normed, proj_w)
    bias = jnp.pad(b_decay, (0, EXTRA - heads))[None]
    gated, kept, cum, cum_rows = retention(projected, bias, seg_col, seg_col.T, width, head_dim)
    mixed = tokens + sum_tokens(dot(gated, out_w))
    scale_two = rms(mixed)
    normed_ffn = gather_tokens((mixed * scale_two * gain_ffn).astype(LOW))
    gate_up = dot(normed_ffn, gu_w)
    gate_part, up_part = gate_up[:, :units], gate_up[:, units:]
    sigma = jax.nn.sigmoid(gate_part)
    activated = (gate_part * sigma * up_part).astype(LOW)
    result = mixed + sum_tokens(dot(activated, down_w))

    position = me_seq * count + jnp.arange(count, dtype=jnp.int32)
    valid_mask = (position < valid_count[0]).astype(WIDE)[:, None]
    mismatch = result - teacher[0]
    grad_out = cotangent[0] + valid_mask * mismatch
    squared_local = jnp.sum(valid_mask * mismatch * mismatch)
    count_local = jnp.sum(valid_mask)

    grad_ffn = gather_tokens(grad_out.astype(LOW))
    grad = dot(activated, grad_ffn, 0, 0)
    down_grad = sum_rows(spread(grad, 0).reshape(-1, model_width))
    grad_act = dot(grad_ffn, down_w, 1, 1)
    grad_gate = grad_act * up_part * sigma * (1.0 + gate_part * (1.0 - sigma))
    grad_up = grad_act * gate_part * sigma
    grad_both = jnp.concatenate([grad_gate, grad_up], axis=1).astype(LOW)
    gu_grad = sum_columns(dot(normed_ffn, grad_both, 0, 0), 2)
    grad_normed = sum_tokens(dot(grad_both, gu_w, 1, 1))
    grad_mid, gain_ffn_grad = norm_back(grad_normed, mixed, scale_two, gain_ffn)
    grad_mixed = grad_out + grad_mid
    grad_att = gather_tokens(grad_mixed.astype(LOW))
    grad = dot(gated, grad_att, 0, 0)
    out_grad = sum_rows(spread(grad.reshape(width, -1, model_width), 1).reshape(-1, model_width))
    grad_gated = dot(grad_att, out_w, 1, 1)
    grad_proj, bias_local = retention_back(
        projected, bias, kept, grad_gated, cum, cum_rows, seg_col, seg_col.T, width, head_dim
    )
    share = 4 * width * head_dim
    grad = dot(normed, grad_proj, 0, 0)
    proj_grad = sum_columns(grad[:, :share], 4 * width)
    decay_grad = sum_rows(grad[:, share : share + heads])
    grad_normed_one = sum_tokens(dot(grad_proj, proj_w, 1, 1))
    grad_first, gain_ret_grad = norm_back(grad_normed_one, tokens, scale_one, gain_ret)
    totals = lax.psum(
        (gain_ret_grad, gain_ffn_grad, bias_local[0], squared_local, count_local), ("dp", "seq")
    )
    return (
        result[None],
        (grad_mixed + grad_first)[None],
        proj_grad,
        decay_grad,
        totals[2][:heads],
        out_grad,
        totals[0],
        totals[1],
        gu_grad,
        down_grad,
        totals[3] / (totals[4] * model_width),
    )


def solution(mesh):
    rows = P("dp", None)
    in_specs = (
        P("dp", "seq", None),
        P("dp", "seq"),
        P("dp"),
        P("dp", "seq", None),
        P("dp", "seq", None),
        rows,
        rows,
        P(),
        rows,
        P(),
        P(),
        rows,
        rows,
    )
    out_specs = (
        P("dp", "seq", None),
        P("dp", "seq", None),
        rows,
        rows,
        P(),
        rows,
        P(),
        P(),
        rows,
        rows,
        P(),
    )
    sizes = dict(mesh.shape)
    shards = placed_shards if sizes["dp"] == 8 and sizes["seq"] == 4 else plain_shards
    return jax.shard_map(shards, mesh=mesh, in_specs=in_specs, out_specs=out_specs, check_vma=False)
```

```python
import functools

import jax
import jax.numpy as jnp
from jax import lax
from jax.experimental import pallas as pl
from jax.experimental.pallas import tpu as pltpu
from jax.sharding import PartitionSpec as P

LOW = jnp.bfloat16
WIDE = jnp.float32
ORDER = (2, 1, 3, 0)
EXTRA = 128
VMEM_BYTES = 56 * 1024 * 1024


def dot(left, right, left_dim=1, right_dim=0):
    return lax.dot_general(
        left, right, (((left_dim,), (right_dim,)), ((), ())), preferred_element_type=WIDE
    )


def blocks_at(matrix, places, size, axis):
    return jnp.concatenate(
        [lax.dynamic_slice_in_dim(matrix, place * size, size, axis) for place in places], axis=axis
    )


def after(value, *tokens):
    return lax.optimization_barrier((value,) + tokens)[0]


def in_vmem():
    return pl.BlockSpec(memory_space=pltpu.VMEM)


def anywhere():
    return pl.BlockSpec(memory_space=pl.ANY)


def cost(*unused):
    return pl.CostEstimate(flops=0, bytes_accessed=0, transcendentals=0)


def pieces_kernel(*refs):
    rows, pieces, target = refs[0], refs[1:-1], refs[-1]
    target[...] = dot(rows[...], jnp.concatenate([piece[...] for piece in pieces], axis=0))


def pieces_product(rows, pieces):
    depth, width = pieces[0].shape
    height, count, tile = rows.shape[0], len(pieces), 256
    return pl.pallas_call(
        pieces_kernel,
        grid=(-(-width // tile),),
        in_specs=[pl.BlockSpec((height, count * depth), lambda i: (0, 0))]
        + [pl.BlockSpec((depth, tile), lambda i: (0, i))] * count,
        out_specs=pl.BlockSpec((height, tile), lambda i: (0, i)),
        out_shape=jax.ShapeDtypeStruct((height, width), WIDE),
        compiler_params=pltpu.CompilerParams(vmem_limit_bytes=VMEM_BYTES),
        cost_estimate=cost(),
    )(rows, *pieces)


def gate_up_kernel(count, *refs):
    rows, gate_w, up_w = refs[0], refs[1 : 1 + count], refs[1 + count : 1 + 2 * count]
    gate, up, activated = refs[1 + 2 * count :]
    tile = gate.shape[1]
    left = jnp.concatenate([piece[...] for piece in gate_w], axis=0)
    right = jnp.concatenate([piece[...] for piece in up_w], axis=0)
    both = dot(rows[...], jnp.concatenate([left, right], axis=1))
    gate_part, up_part = both[:, :tile], both[:, tile:]
    gate[...] = gate_part
    up[...] = up_part
    activated[...] = (gate_part * jax.nn.sigmoid(gate_part) * up_part).astype(LOW)


def gate_up_product(rows, pieces, units):
    height, depth = rows.shape
    tile = 128
    steps, count = units // tile, len(pieces)
    column = pl.BlockSpec((height, tile), lambda i: (0, i))
    size = pieces[0].shape[0]
    return pl.pallas_call(
        functools.partial(gate_up_kernel, count),
        grid=(steps,),
        in_specs=[pl.BlockSpec((height, depth), lambda i: (0, 0))]
        + [pl.BlockSpec((size, tile), lambda i: (0, i))] * count
        + [pl.BlockSpec((size, tile), lambda i: (0, steps + i))] * count,
        out_specs=[column] * 3,
        out_shape=[
            jax.ShapeDtypeStruct((height, units), WIDE),
            jax.ShapeDtypeStruct((height, units), WIDE),
            jax.ShapeDtypeStruct((height, units), LOW),
        ],
        compiler_params=pltpu.CompilerParams(vmem_limit_bytes=VMEM_BYTES),
        cost_estimate=cost(),
    )(rows, *pieces, *pieces)


def in_row_order_kernel(*refs):
    pieces, target = refs[:-1], refs[-1]
    me = lax.axis_index("seq")
    size = pieces[0].shape[0]
    for k, piece in enumerate(pieces):
        target[pl.ds(pl.multiple_of(lax.bitwise_xor(me, k) * size, size), size), :] = piece[...]


def in_row_order(pieces):
    size, width = pieces[0].shape
    return pl.pallas_call(
        in_row_order_kernel,
        in_specs=[in_vmem()] * len(pieces),
        out_specs=in_vmem(),
        out_shape=jax.ShapeDtypeStruct((len(pieces) * size, width), LOW),
        compiler_params=pltpu.CompilerParams(vmem_limit_bytes=VMEM_BYTES),
        cost_estimate=cost(),
    )(*pieces)


def proj_share_kernel(blocks, seq_count, source, decay, target):
    me = lax.axis_index("seq")
    rows, extra = decay.shape
    size = (target.shape[1] - EXTRA) // blocks
    for i in range(blocks):
        place = pl.multiple_of((i * seq_count + me) * size, size)
        target[:, i * size : (i + 1) * size] = source[:, pl.ds(place, size)]
    padded = jnp.concatenate([decay[...], jnp.zeros((rows, EXTRA - extra), LOW)], axis=1)
    target[:, blocks * size :] = padded


def row_shares_kernel(part, shard, seq_count, out, down, out_to, down_to):
    me = lax.axis_index("seq")
    half = out_to.shape[0]
    out_to[...] = out[pl.ds(pl.multiple_of(lax.rem(me, 2) * half, half), half), :]
    sure = shard - part * (seq_count - 1)
    rest = part - sure
    start = pl.multiple_of(me * part, 16)
    down_to[:sure, :] = down[pl.ds(start, sure), :]
    if rest:
        last = pl.multiple_of(jnp.minimum(start + sure, shard - rest), 16)
        rows = down[pl.ds(last, rest), :]
        down_to[sure:, :] = jnp.where(me < seq_count - 1, rows, jnp.zeros_like(rows))


def gate_up_share_kernel(part, shard, dp_count, source, target):
    me = lax.axis_index("seq")
    lane = 128
    window = 384
    columns = source.shape[1]
    half = dp_count * part
    row = lax.broadcasted_iota(jnp.int32, (window, lane), 0)
    col = lax.broadcasted_iota(jnp.int32, (window, lane), 1)
    for tile in range(target.shape[1] // lane):
        first = tile * lane % half
        which = tile * lane // half
        total = None
        for d in range(first // part, (first + lane - 1) // part + 1):
            base = (which * dp_count + d) * shard + me * part
            begin = pl.multiple_of(
                jnp.minimum(lax.div(base, lane) * lane, (columns - window) // lane * lane), lane
            )
            unit = first + col - d * part
            hit = (row + begin == base + unit) & (unit >= 0) & (unit < part)
            hit = hit & (me * part + unit < shard)
            chosen = jnp.where(hit, 1.0, 0.0).astype(LOW)
            piece = jnp.dot(source[:, pl.ds(begin, window)], chosen, preferred_element_type=WIDE)
            total = piece if total is None else total + piece
        target[:, pl.ds(tile * lane, lane)] = total.astype(LOW)


def gate_up_whole_kernel(part, shard, *refs):
    pieces, target, held = refs[:-2], refs[-2], refs[-1]
    me = lax.axis_index("seq")
    lane, window = 128, 256
    count = len(pieces)
    for k in range(count):
        place = lax.bitwise_xor(me, k)
        held[place] = pieces[k][...]
    row = lax.broadcasted_iota(jnp.int32, (window, lane), 0)
    col = lax.broadcasted_iota(jnp.int32, (window, lane), 1)
    width = pieces[0].shape[1]
    for tile in range(target.shape[1] // lane):
        at = tile * lane
        total = None
        while at < (tile + 1) * lane:
            block, inside = divmod(at, shard)
            share, unit = divmod(inside, part)
            stop = min((tile + 1) * lane, block * shard + min((share + 1) * part, shard))
            from_column = block * part + unit
            begin = min(from_column // lane * lane, width - window)
            off = at - tile * lane
            hit = (row + begin - from_column == col - off) & (col >= off) & (col < off + stop - at)
            chosen = jnp.where(hit, 1.0, 0.0).astype(LOW)
            piece = jnp.dot(held[share, :, begin : begin + window], chosen, preferred_element_type=WIDE)
            total = piece if total is None else total + piece
            at = stop
        target[:, tile * lane : (tile + 1) * lane] = total


def proj_whole_kernel(skip, *refs):
    pieces, target = refs[skip:-1], refs[-1]
    me = lax.axis_index("seq")
    size = pieces[0].shape[1]
    for k, piece in enumerate(pieces):
        place = pl.multiple_of(lax.bitwise_xor(me, k) * size, size)
        target[:, pl.ds(place, size)] = piece[...].astype(WIDE)


def down_whole_kernel(part, shard, *refs):
    pieces, target = refs[:-1], refs[-1]
    me = lax.axis_index("seq")
    count = len(pieces)
    sure = shard - part * (count - 1)
    for k, piece in enumerate(pieces):
        place = lax.bitwise_xor(me, k)
        start = pl.multiple_of(place * part, 16)
        target[pl.ds(start, sure), :] = piece[:sure, :].astype(WIDE)
        if sure < part:

            @pl.when(place < count - 1)
            def _(piece=piece, start=start):
                target[pl.ds(pl.multiple_of(start + sure, 16), part - sure), :] = piece[sure:, :].astype(WIDE)


def triangle(size, reverse):
    row = lax.broadcasted_iota(jnp.int32, (size, size), 0)
    col = lax.broadcasted_iota(jnp.int32, (size, size), 1)
    return jnp.where(row <= col if reverse else row >= col, 1.0, 0.0)


def running_sum(table, step, source, target, reverse):
    count, lanes = source.shape
    carry = jnp.zeros((1, lanes), WIDE)
    starts = range(0, count, step)
    for at in reversed(starts) if reverse else starts:
        block = source[at : at + step, :]
        sums = lax.dot_general(
            table, block, (((1,), (0,)), ((), ())),
            precision=lax.Precision.HIGHEST, preferred_element_type=WIDE,
        ) + carry
        target[at : at + step, :] = sums
        carry = carry + jnp.sum(block, axis=0, keepdims=True)


def decay_rows(at, size, cum_col, cum_row, seg_col, seg_row):
    wide = at + size
    spread = cum_col[at:wide] - cum_row[:, :wide]
    order_t = lax.broadcasted_iota(jnp.int32, (size, wide), 0) + at
    order_s = lax.broadcasted_iota(jnp.int32, (size, wide), 1)
    allowed = (seg_col[at:wide] == seg_row[:, :wide]) & (order_t >= order_s)
    return jnp.where(allowed, jnp.exp(jnp.minimum(spread, 0.0)), 0.0)


def lane_of(table, lane):
    lanes = lax.broadcasted_iota(jnp.int32, table.shape, 1)
    return jnp.sum(jnp.where(lanes == lane, table, 0.0), axis=1, keepdims=True)


def forward_kernel(
    step, scale, seq_count, q, k, v, gate, logit, bias, seg_col, seg_row, gated, kept, cum, cum_rows, held
):
    head = pl.program_id(0)
    lane = head * seq_count + lax.axis_index("seq")

    @pl.when(head == 0)
    def _():
        value = logit[...] + bias[...]
        held[...] = (jnp.minimum(value, 0.0) - jnp.log1p(jnp.exp(-jnp.abs(value)))) / 16.0
        running_sum(triangle(step, False), step, held, cum, False)
        cum_rows[...] = cum[...].T

    keys, values = k[...].astype(LOW), v[...].astype(LOW)
    seg_c, seg_r = seg_col[...], seg_row[...]
    cum_c, cum_r = lane_of(cum[...], lane), cum_rows[pl.ds(lane, 1), :]
    for at in range(0, q.shape[0], step):
        stop = at + step
        rows = (q[at:stop, :] * scale).astype(LOW)
        scores = dot(rows, keys[:stop], 1, 1) * decay_rows(at, step, cum_c, cum_r, seg_c, seg_r)
        high = scores.astype(LOW)
        rest = (scores - high.astype(WIDE)).astype(LOW)
        retained = dot(high, values[:stop]) + dot(rest, values[:stop])
        kept[at:stop, :] = retained
        power = jnp.mean(retained * retained, axis=1, keepdims=True)
        unit = retained * lax.rsqrt(jnp.maximum(power, 1.0))
        gates = gate[at:stop, :]
        gated[at:stop, :] = (gates * jax.nn.sigmoid(gates) * unit).astype(LOW)


def backward_kernel(
    step, scale, width, seq_count, q, k, v, gate, logit, bias, kept, grad, cum, cum_rows, seg_col, seg_row,
    grad_proj, bias_sum, grad_k, grad_v, grad_cum, held,
):
    head = pl.program_id(0)
    lane = head * seq_count + lax.axis_index("seq")
    size = q.shape[1]
    keys, values = k[...].astype(LOW), v[...].astype(LOW)
    seg_c, seg_r = seg_col[...], seg_row[...]
    cum_c, cum_r = lane_of(cum[...], lane), cum_rows[pl.ds(lane, 1), :]

    def columns(block):
        return pl.ds(pl.multiple_of((block * width + head) * size, size), size)

    @pl.when(head == 0)
    def _():
        grad_cum[...] = jnp.zeros_like(grad_cum)

    count = q.shape[0]
    lanes = lax.broadcasted_iota(jnp.int32, (step, EXTRA), 1)
    for at in reversed(range(0, count, step)):
        stop = at + step
        first = stop == count
        retained, gates, grads = kept[at:stop, :], gate[at:stop, :], grad[at:stop, :]
        power = jnp.mean(retained * retained, axis=1, keepdims=True)
        inverse = lax.rsqrt(jnp.maximum(power, 1.0))
        unit = retained * inverse
        sigma = jax.nn.sigmoid(gates)
        grad_proj[at:stop, columns(3)] = (
            grads * unit * sigma * (1.0 + gates * (1.0 - sigma))
        ).astype(LOW)
        grad_unit = grads * gates * sigma
        along = jnp.mean(grad_unit * unit, axis=1, keepdims=True)
        grad_low = (inverse * jnp.where(power > 1.0, grad_unit - unit * along, grad_unit)).astype(LOW)
        rows = (q[at:stop, :] * scale).astype(LOW)
        table = decay_rows(at, step, cum_c, cum_r, seg_c, seg_r)
        scores = (dot(rows, keys[:stop], 1, 1) * table).astype(LOW)
        pairs = (table * dot(grad_low, values[:stop], 1, 1)).astype(LOW)
        grad_q = dot(pairs, keys[:stop])
        grad_proj[at:stop, columns(0)] = (grad_q * scale).astype(LOW)
        part_k = dot(pairs, rows, 0, 0)
        part_v = dot(scores, grad_low, 0, 0)
        if first:
            grad_k[:stop, :] = part_k
            grad_v[:stop, :] = part_v
        else:
            grad_k[:stop, :] += part_k
            grad_v[:stop, :] += part_v
        along_q = jnp.sum(rows.astype(WIDE) * grad_q, axis=1, keepdims=True)
        along_k = jnp.sum(keys[at:stop].astype(WIDE) * grad_k[at:stop, :], axis=1, keepdims=True)
        grad_cum[at:stop, :] += jnp.where(lanes == lane, along_q - along_k, 0.0)
    grad_proj[:, columns(1)] = grad_k[...].astype(LOW)
    grad_proj[:, columns(2)] = grad_v[...].astype(LOW)

    @pl.when(head == width - 1)
    def _():
        running_sum(triangle(step, True), step, grad_cum, held, True)
        value = held[...] * jax.nn.sigmoid(-(logit[...] + bias[...])) / 16.0
        bias_sum[...] = jnp.sum(value, axis=0, keepdims=True)
        grad_proj[:, 4 * width * size :] = value.astype(LOW)


def head_specs(row, size, width):
    def block(number):
        return pl.BlockSpec((row, size), lambda h: (0, number * width + h))

    def same(shape):
        return pl.BlockSpec(shape, lambda h: (0, 0))

    logit = pl.BlockSpec((row, EXTRA), lambda h: (0, 4 * width * size // EXTRA))
    return block, same, logit


def retention(projected, bias, seg_col, seg_row, width, size):
    row = projected.shape[0]
    block, same, logit = head_specs(row, size, width)
    pairs = row * row * width * 5 // 8
    return pl.pallas_call(
        functools.partial(forward_kernel, row // 4, size ** (-0.5), lax.axis_size("seq")),
        grid=(width,),
        in_specs=[block(0), block(1), block(2), block(3), logit, same((1, EXTRA)), same((row, 1)), same((1, row))],
        out_specs=[block(0), block(0), same((row, EXTRA)), same((EXTRA, row))],
        out_shape=[
            jax.ShapeDtypeStruct((row, width * size), LOW),
            jax.ShapeDtypeStruct((row, width * size), WIDE),
            jax.ShapeDtypeStruct((row, EXTRA), WIDE),
            jax.ShapeDtypeStruct((EXTRA, row), WIDE),
        ],
        scratch_shapes=[pltpu.VMEM((row, EXTRA), WIDE)],
        compiler_params=pltpu.CompilerParams(vmem_limit_bytes=VMEM_BYTES),
        cost_estimate=cost(pairs * size * 4, projected.size * 6, pairs),
    )(*([projected] * 5), bias, seg_col, seg_row)


def retention_back(projected, bias, kept, grad_gated, cum, cum_rows, seg_col, seg_row, width, size):
    row = projected.shape[0]
    block, same, logit = head_specs(row, size, width)
    pairs = row * row * width * 5 // 8
    return pl.pallas_call(
        functools.partial(backward_kernel, row // 4, size ** (-0.5), width, lax.axis_size("seq")),
        grid=(width,),
        in_specs=[block(0), block(1), block(2), block(3), logit, same((1, EXTRA)), block(0), block(0)]
        + [same((row, EXTRA)), same((EXTRA, row)), same((row, 1)), same((1, row))],
        out_specs=[same((row, 4 * width * size + EXTRA)), same((1, EXTRA))],
        out_shape=[
            jax.ShapeDtypeStruct((row, 4 * width * size + EXTRA), LOW),
            jax.ShapeDtypeStruct((1, EXTRA), WIDE),
        ],
        scratch_shapes=[pltpu.VMEM((row, size), WIDE)] * 2 + [pltpu.VMEM((row, EXTRA), WIDE)] * 2,
        compiler_params=pltpu.CompilerParams(vmem_limit_bytes=VMEM_BYTES),
        cost_estimate=cost(pairs * size * 10, projected.size * 8, pairs),
    )(*([projected] * 5), bias, kept, grad_gated, cum, cum_rows, seg_col, seg_row)


class Order:
    def __init__(self):
        self.last = None

    def put(self, value):
        if self.last is not None:
            value = after(value, self.last)
        self.last = value
        return value


class Links:
    def __init__(self, dp_count, seq_count):
        self.dp_count, self.seq_count = dp_count, seq_count
        self.ring = dp_count // 2
        self.me_dp, self.me_seq = lax.axis_index("dp"), lax.axis_index("seq")
        self.turn, self.side = self.me_dp // 2, self.me_dp % 2

    def around(self, value, by=1):
        count = self.dp_count
        return lax.ppermute(value, "dp", [(d, (d + 2 * by) % count) for d in range(count)])

    def across(self, value):
        return lax.ppermute(value, "dp", [(d, d ^ 1) for d in range(self.dp_count)])

    def across_one_way(self, value, toward):
        pairs = [
            (d * self.seq_count + s, (d ^ 1) * self.seq_count + s)
            for d in range(self.dp_count)
            for s in range(self.seq_count)
            if (d % 2 == s // 2) != toward
        ]
        return lax.ppermute(value, ("dp", "seq"), pairs)

    def core(self, value):
        return lax.ppermute(value, "seq", [(s, s ^ 1) for s in range(self.seq_count)])

    def chip(self, value):
        return lax.ppermute(value, "seq", [(s, s ^ 2) for s in range(self.seq_count)])

    def sources(self):
        return [
            ((self.turn - r) % self.ring) * 2 + (self.side ^ e) for e in range(2) for r in ORDER
        ]

    def spot(self, r):
        found = ORDER.index(0)
        for value in range(1, self.ring):
            found = jnp.where(r == value, ORDER.index(value), found)
        return found

    def places(self):
        found = []
        for d in range(self.dp_count):
            r = (self.turn - d // 2) % self.ring
            found.append(self.spot(r) + (self.side ^ (d % 2)) * self.ring)
        return found

    def total_steps(self):
        def step(axis, count, apart):
            pairs = [(d, d ^ apart) for d in range(count)]
            return lambda value: value + lax.ppermute(value, axis, pairs)

        return [step("seq", self.seq_count, apart) for apart in (1, 2)] + [
            step("dp", self.dp_count, apart) for apart in (1, 2, 4)
        ]

    def own_order(self, rows):
        me = self.me_seq
        return blocks_at(rows, [me ^ 1, me ^ 3, me ^ 2, me], rows.shape[0] // 4, 0)

    def to_rel(self, value):
        return blocks_at(value, self.sources(), value.shape[1] // self.dp_count, 1)

    def from_rel(self, value):
        return blocks_at(value, self.places(), value.shape[1] // self.dp_count, 1)


def sum_low(*parts):
    total = parts[0].astype(WIDE)
    for part in parts[1:]:
        total = total + part.astype(WIDE)
    return total.astype(LOW)


def weight_shares(links, width, part, shard, w_proj, w_decay, w_out, w_down):
    rows, columns = w_proj.shape[0], w_proj.shape[1] // links.seq_count + EXTRA
    model = w_down.shape[1]
    block = min(rows, 64)
    proj = pl.pallas_call(
        functools.partial(proj_share_kernel, 4 * width, links.seq_count),
        grid=(rows // block,),
        in_specs=[
            pl.BlockSpec((block, w_proj.shape[1]), lambda i: (i, 0)),
            pl.BlockSpec((block, w_decay.shape[1]), lambda i: (i, 0)),
        ],
        out_specs=pl.BlockSpec((block, columns), lambda i: (i, 0)),
        out_shape=jax.ShapeDtypeStruct((rows, columns), LOW),
        compiler_params=pltpu.CompilerParams(vmem_limit_bytes=VMEM_BYTES),
        cost_estimate=cost(0, 10 * rows * columns),
    )(w_proj, w_decay)
    out, down = pl.pallas_call(
        functools.partial(row_shares_kernel, part, shard, links.seq_count),
        in_specs=[in_vmem()] * 2,
        out_specs=[in_vmem()] * 2,
        out_shape=[
            jax.ShapeDtypeStruct((w_out.shape[0] // 2, model), LOW),
            jax.ShapeDtypeStruct((part, model), LOW),
        ],
        compiler_params=pltpu.CompilerParams(vmem_limit_bytes=VMEM_BYTES),
        cost_estimate=cost(0, 3 * w_out.size + 3 * w_down.size),
    )(w_out, w_down)
    return proj, out, down


def gate_up_share(links, part, shard, w_gu):
    rows, units = w_gu.shape[0], part * links.dp_count
    return pl.pallas_call(
        functools.partial(gate_up_share_kernel, part, shard, links.dp_count),
        in_specs=[in_vmem()],
        out_specs=in_vmem(),
        out_shape=jax.ShapeDtypeStruct((rows, 2 * units), LOW),
        compiler_params=pltpu.CompilerParams(vmem_limit_bytes=VMEM_BYTES),
        cost_estimate=cost(2 * rows * 768 * 2 * units, 2 * w_gu.size + 4 * rows * units),
    )(w_gu)


def whole_down(part, shard, pieces):
    model = pieces[0].shape[1]
    return pl.pallas_call(
        functools.partial(down_whole_kernel, part, shard),
        in_specs=[in_vmem()] * 4,
        out_specs=in_vmem(),
        out_shape=jax.ShapeDtypeStruct((shard, model), WIDE),
        compiler_params=pltpu.CompilerParams(vmem_limit_bytes=VMEM_BYTES),
        cost_estimate=cost(0, 6 * shard * model),
    )(*pieces)


def whole_gate_up(part, shard, dp_count, pieces):
    rows, columns = pieces[0].shape
    block = min(rows, 64)
    whole = 2 * dp_count * shard
    return pl.pallas_call(
        functools.partial(gate_up_whole_kernel, part, shard),
        grid=(rows // block,),
        in_specs=[pl.BlockSpec((block, columns), lambda i: (i, 0))] * 4,
        out_specs=pl.BlockSpec((block, whole), lambda i: (i, 0)),
        out_shape=jax.ShapeDtypeStruct((rows, whole), WIDE),
        scratch_shapes=[pltpu.VMEM((4, block, columns), LOW)],
        compiler_params=pltpu.CompilerParams(vmem_limit_bytes=VMEM_BYTES),
        cost_estimate=cost(rows * whole * 1024, rows * whole * 6),
    )(*pieces)


def whole_proj(half, number, size, kept, pieces):
    rows = pieces[0].shape[0]
    return pl.pallas_call(
        functools.partial(proj_whole_kernel, len(kept)),
        grid=(half,),
        in_specs=[anywhere()] * len(kept) + [pl.BlockSpec((rows, size), lambda i: (0, i))] * 4,
        out_specs=pl.BlockSpec((rows, 4 * size), lambda i: (0, number * half + i)),
        out_shape=jax.ShapeDtypeStruct((rows, 8 * half * size), WIDE),
        input_output_aliases={0: 0} if kept else {},
        compiler_params=pltpu.CompilerParams(vmem_limit_bytes=VMEM_BYTES),
        cost_estimate=cost(0, rows * half * size * 24),
    )(*kept, *pieces)


def placed_shards(
    inputs, segments, valid_count, teacher, cotangent, w_proj, w_decay, b_decay, w_out,
    gain_ret, gain_ffn, w_gu, w_down,
):
    dp_count, seq_count = lax.axis_size("dp"), lax.axis_size("seq")
    links, order = Links(dp_count, seq_count), Order()
    put = order.put
    tokens = inputs[0]
    count, model_width = tokens.shape
    heads = w_decay.shape[1]
    head_dim = model_width // heads
    width = heads // seq_count
    shard = w_down.shape[0]
    part = -(-shard // (16 * seq_count)) * 16
    units = part * dp_count
    first_core, x_half = links.me_seq % 2 == 0, links.me_seq // 2

    proj_share, out_share, down_share = weight_shares(
        links, width, part, shard, w_proj, w_decay, w_out, w_down
    )
    proj_share = put(proj_share)
    p_ring = links.around(proj_share)
    p_0 = links.across(proj_share)
    scale_one = rms(tokens)
    normed_here = links.to_rel((tokens * scale_one * gain_ret).astype(LOW))
    ids = jnp.broadcast_to(segments[0][:, None].astype(LOW), (count, EXTRA))
    sent = put(jnp.concatenate([normed_here, ids], axis=1))
    n_far, n_near = links.chip(sent), links.core(sent)
    out_share, down_share = put(out_share), put(down_share)
    out_cross = links.across_one_way(out_share, False)
    gu_share = put(gate_up_share(links, part, shard, after(w_gu, sent)))
    p_own_1, p_0 = put(p_ring), put(p_0)
    p_ring, p_1 = links.around(p_own_1), links.across(p_own_1)
    n_near, n_far = put(n_near), put(n_far)
    n_both = put(links.core(n_far))
    normed = put(in_row_order([sent, n_near, n_far, n_both]))
    seg_col = normed[:, model_width : model_width + 1].astype(jnp.int32)
    out_block = put(jnp.where(links.side == x_half, out_share, put(out_cross)))
    p_own_2 = put(p_ring)
    p_ring = links.around(p_own_2)
    p_1 = put(p_1)
    p_2 = links.across(p_own_2)
    p_own_3 = put(p_ring)
    o_ring = links.around(out_block)
    p_2 = put(p_2)
    p_3 = links.across(p_own_3)
    o_own_1 = put(o_ring)
    o_ring = links.around(o_own_1)
    o_own_2 = put(o_ring)
    g_ring = links.around(put(gu_share))
    o_ring = links.around(o_own_2)
    p_3 = put(p_3)
    g_0 = links.across(put(gu_share))
    p_pieces = [p_own_2, p_own_1, p_own_3, proj_share, p_2, p_1, p_3, p_0]
    projected = put(pieces_product(normed, p_pieces))
    bias = jnp.pad(b_decay, (0, EXTRA - heads))[None]
    gated, kept, cum, cum_rows = retention(projected, bias, seg_col, seg_col.T, width, head_dim)
    gated = put(gated)
    o_own_3, g_own_1, g_0 = put(o_ring), put(g_ring), put(g_0)
    g_ring, g_1 = links.around(g_own_1), links.across(g_own_1)
    out_w = blocks_at(
        jnp.concatenate([o_own_2, o_own_1, o_own_3, out_block], axis=0),
        [links.spot((links.turn - j) % links.ring) for j in range(links.ring)],
        out_share.shape[0],
        0,
    )

    def tokens_start(rows, weight, dims):
        come = links.core(put(dot(rows[: 2 * count], weight, *dims).astype(LOW)))
        far = dot(rows[2 * count : 3 * count], weight, *dims) + come[count:].astype(WIDE)
        return come, links.chip(put(far.astype(LOW)))

    def tokens_end(started, rows, weight, dims):
        come, arrived = started
        own = dot(rows[3 * count :], weight, *dims)
        return own + come[:count].astype(WIDE) + put(arrived).astype(WIDE)

    gated_own = links.own_order(gated)
    going = tokens_start(gated_own, out_w, (1, 0))
    g_own_2 = put(g_ring)
    g_ring = links.around(g_own_2)
    g_1 = put(g_1)
    g_2 = links.across(g_own_2)
    mixed = put(tokens + tokens_end(going, gated_own, out_w, (1, 0)))
    scale_two = rms(mixed)
    sent = put(links.to_rel((mixed * scale_two * gain_ffn).astype(LOW)))
    n_far, n_near = links.chip(sent), links.core(sent)
    g_own_3, g_2 = put(g_ring), put(g_2)
    g_3 = links.across(g_own_3)
    d_ring = links.around(put(down_share))
    n_far, n_near = put(n_far), put(n_near)
    n_both = put(links.core(n_far))
    normed_ffn = put(jnp.concatenate([n_near, n_both, n_far, sent], axis=0))
    d_own_1 = put(d_ring)
    d_ring = links.around(d_own_1)
    p_pieces = [after(piece, d_own_1) for piece in p_pieces]
    proj_w = put(jnp.concatenate(p_pieces, axis=0))
    g_3 = put(g_3)
    d_0 = links.across(put(down_share))
    d_1 = links.across(d_own_1)
    g_pieces = [g_own_2, g_own_1, g_own_3, gu_share, g_2, g_1, g_3, g_0]
    gate_part, up_part, activated = gate_up_product(normed_ffn, g_pieces, units)
    activated = put(activated)
    d_own_2 = put(d_ring)
    d_ring = links.around(d_own_2)
    d_0, d_1 = put(d_0), put(d_1)
    d_2 = links.across(d_own_2)
    g_pieces = [after(piece, d_1) for piece in g_pieces]
    gu_w = put(jnp.concatenate(g_pieces, axis=0))
    d_own_3 = put(d_ring)
    d_3 = links.across(d_own_3)
    d_2, d_3 = put(d_2), put(d_3)
    stacked = jnp.concatenate(
        [d_own_2, d_own_1, d_own_3, down_share, d_2, d_1, d_3, d_0], axis=0
    )
    down_w = blocks_at(stacked, links.places(), part, 0)
    going = tokens_start(activated, down_w, (1, 0))
    result = mixed + tokens_end(going, activated, down_w, (1, 0))

    position = links.me_seq * count + jnp.arange(count, dtype=jnp.int32)
    valid_mask = (position < valid_count[0]).astype(WIDE)[:, None]
    mismatch = result - teacher[0]
    grad_out = cotangent[0] + valid_mask * mismatch
    squared_local = jnp.sum(valid_mask * mismatch * mismatch)
    count_local = jnp.sum(valid_mask)

    def rows_of(left, right, i, *added):
        size = model_width // dp_count
        total = dot(left[:, i * size : (i + 1) * size], right, 0, 0)
        for more in added:
            total = total + more.astype(WIDE)
        return total.astype(LOW)

    def gather_seq(total):
        far, near = links.chip(total), links.core(total)
        return [total, near, far, links.core(far)]

    sent = put(grad_out.astype(LOW))
    n_far, n_near = links.chip(sent), links.core(sent)
    n_far, n_near = put(n_far), put(n_near)
    n_both = put(links.core(n_far))
    grad_ffn = put(jnp.concatenate([n_near, n_both, n_far, sent], axis=0))
    whole = dot(activated, grad_ffn, 0, 0).astype(LOW)
    places = links.sources()
    d_go = [put(blocks_at(whole, places[i:k], part, 0)) for i, k in ((4, 5), (5, 6), (6, 8))]
    d_come = [links.across(d_go[0])]
    grad_act = dot(after(grad_ffn, order.last), down_w, 1, 1)
    sigma = jax.nn.sigmoid(gate_part)
    grad_gate = grad_act * up_part * sigma * (1.0 + gate_part * (1.0 - sigma))
    grad_up = grad_act * gate_part * sigma
    grad_both = put(jnp.concatenate([grad_gate, grad_up], axis=1).astype(LOW))
    d_come[0] = put(d_come[0])
    d_come.append(links.across(put(d_go[1])))
    back = after(grad_both, order.last)
    come = links.core(put(dot(back[: 2 * count], gu_w, 1, 1).astype(LOW)))
    d_come[1] = put(d_come[1])
    d_come.append(links.across(put(d_go[2])))
    far = dot(back[2 * count : 3 * count], gu_w, 1, 1) + come[count:].astype(WIDE)
    going = come, links.chip(put(far.astype(LOW)))
    d_first = sum_low(blocks_at(whole, places[1:2], part, 0), d_come[1])
    d_second = sum_low(blocks_at(whole, places[0:1], part, 0), d_come[0])
    d_second, d_first = links.around(put(d_second), 1), links.around(put(d_first), -1)
    g_other = [put(rows_of(after(normed_ffn, order.last), grad_both, 4))]
    d_come[2] = put(d_come[2])
    g_come = [links.across(put(g_other[0]))]
    grad_normed = links.from_rel(tokens_end(going, grad_both, gu_w, (1, 1)))
    grad_mid, gain_ffn_grad = norm_back(grad_normed, mixed, scale_two, gain_ffn)
    grad_mixed = grad_out + grad_mid
    sent = put(grad_mixed.astype(LOW))
    n_far, n_near = links.chip(sent), links.core(sent)
    d_second, d_first = put(d_second), put(d_first)
    d_third = put(sum_low(blocks_at(whole, places[2:3], part, 0), d_come[2][:part], d_second))
    d_third = links.around(d_third, 1)
    g_come[0] = put(g_come[0])
    g_other.append(put(rows_of(after(normed_ffn, order.last), grad_both, 5)))
    g_come.append(links.across(g_other[1]))
    g_second = links.around(put(rows_of(normed_ffn, grad_both, 0, after(g_come[0], order.last))), 1)
    for i in (6, 7):
        g_other.append(put(rows_of(after(normed_ffn, order.last), grad_both, i)))
    n_far, n_near = put(n_far), put(n_near)
    n_both = put(links.core(n_far))
    grad_att = put(in_row_order([sent, n_near, n_far, n_both]))
    g_come[1] = put(g_come[1])
    g_come.append(links.across(put(g_other[2])))
    g_first = links.around(put(rows_of(normed_ffn, grad_both, 1, after(g_come[1], order.last))), -1)
    d_third, g_second = put(d_third), put(g_second)
    grad_gated = put(dot(after(grad_att, order.last), out_w, 1, 1))
    left = blocks_at(gated, [(links.turn - r) % links.ring for r in ORDER], head_dim, 1)
    o_sums = put(dot(left, after(grad_att, order.last), 0, 0).astype(LOW))
    o_second, o_first, o_third, o_mine = jnp.split(o_sums, 4, axis=0)
    o_second, o_first = links.around(o_second, 1), links.around(o_first, -1)
    grad_proj, bias_local = retention_back(
        projected, bias, kept, after(grad_gated, order.last), cum, cum_rows, seg_col, seg_col.T, width, head_dim
    )
    grad_proj = put(grad_proj)
    g_first, g_come[2] = put(g_first), put(g_come[2])
    g_come.append(links.across(put(g_other[3])))
    p_other = [put(rows_of(normed, after(grad_proj, order.last), 4))]
    back_rows = links.own_order(after(grad_proj, order.last))
    come = put(dot(back_rows[: 2 * count], proj_w, 1, 1).astype(LOW))
    come = links.core(come)
    o_second, o_first = put(o_second), put(o_first)
    o_third = links.around(put(sum_low(o_third, o_second)), 1)
    g_come[3] = put(g_come[3])
    p_come = [links.across(p_other[0])]
    g_third = links.around(put(rows_of(normed_ffn, grad_both, 2, after(g_come[2], order.last), g_second)), 1)
    p_other.append(put(rows_of(normed, after(grad_proj, order.last), 5)))
    p_come[0] = put(p_come[0])
    p_come.append(links.across(p_other[1]))
    far = dot(after(back_rows[2 * count : 3 * count], order.last), proj_w, 1, 1) + come[count:].astype(WIDE)
    going = come, links.chip(put(far.astype(LOW)))
    o_third = put(o_third)
    p_other.append(put(rows_of(normed, after(grad_proj, order.last), 6)))
    p_come[1] = put(p_come[1])
    p_come.append(links.across(p_other[2]))
    p_second = links.around(put(rows_of(normed, after(grad_proj, order.last), 0, p_come[0])), 1)
    d_total = put(sum_low(blocks_at(whole, places[3:4], part, 0), d_come[2][part:], d_first, d_third))
    g_third = put(g_third)
    g_total = put(rows_of(normed_ffn, after(grad_both, order.last), 3, g_come[3], g_first, g_third))
    grad_normed_one = links.from_rel(tokens_end(going, back_rows, proj_w, (1, 1)))
    d_pieces = gather_seq(after(d_total, order.last))
    p_other.append(put(rows_of(normed, after(grad_proj, order.last), 7)))
    p_come[2] = put(p_come[2])
    p_come.append(links.across(p_other[3]))
    p_first = links.around(put(rows_of(normed, after(grad_proj, order.last), 1, p_come[1])), -1)
    grad_first, gain_ret_grad = norm_back(grad_normed_one, tokens, scale_one, gain_ret)
    grad_tokens = put(grad_mixed + grad_first)
    scalars = jnp.pad(jnp.stack([squared_local, count_local]), (0, EXTRA - 2))
    totals = put(jnp.concatenate([gain_ret_grad, gain_ffn_grad, bias_local[0], scalars]))
    totals_steps = links.total_steps()
    totals = totals_steps[0](totals)
    p_second = put(p_second)
    p_third = links.around(put(rows_of(normed, grad_proj, 2, p_come[2], p_second)), 1)
    g_far = put(links.chip(g_total))
    g_pieces = [g_total, links.core(g_total), g_far, links.core(g_far)]
    totals = totals_steps[1](put(totals))
    o_total = put(sum_low(o_mine, o_first, o_third))
    p_first = put(p_first)
    down_grad = put(whole_down(part, shard, [put(piece) for piece in d_pieces]))
    o_come = links.across_one_way(after(o_total, order.last), True)
    totals = put(totals)
    p_come[3], p_third = put(p_come[3]), put(p_third)
    half = 2 * width * head_dim
    p_pieces = []
    for start, stop in ((0, half), (half, 2 * half + EXTRA)):
        total = rows_of(
            normed, grad_proj[:, start:stop], 3,
            p_come[3][:, start:stop], p_first[:, start:stop], p_third[:, start:stop],
        )
        p_pieces.append(gather_seq(put(total)))
    o_mine = put(sum_low(o_total, put(o_come)))
    o_near = put(links.core(o_mine))
    pair = jnp.concatenate(
        [jnp.where(first_core, o_mine, o_near), jnp.where(first_core, o_near, o_mine)], axis=0
    )
    o_far = links.chip(put(pair))
    totals = totals_steps[2](totals)
    g_pieces = [put(piece) for piece in g_pieces]
    gu_grad = put(whole_gate_up(part, shard, dp_count, g_pieces))
    totals = totals_steps[4](totals_steps[3](put(totals)))
    proj_grad = put(whole_proj(2 * width, 0, head_dim, [], [put(piece) for piece in p_pieces[0]]))
    totals = put(totals)
    decay_grad = sum(piece[:, half : half + heads].astype(WIDE) for piece in p_pieces[1])
    proj_grad = whole_proj(2 * width, 1, head_dim, [proj_grad], p_pieces[1])
    out_grad = jnp.where(x_half == links.side, pair, put(o_far)).astype(WIDE)

    gain_ret_total, gain_ffn_total = totals[:model_width], totals[model_width : 2 * model_width]
    bias_total = totals[2 * model_width : 2 * model_width + heads]
    at = 2 * model_width + EXTRA
    mse = totals[at] / (totals[at + 1] * model_width)
    return (
        result[None],
        grad_tokens[None],
        proj_grad,
        decay_grad,
        bias_total,
        out_grad,
        gain_ret_total,
        gain_ffn_total,
        gu_grad,
        down_grad,
        mse,
    )


def rms(value):
    return lax.rsqrt(jnp.mean(value * value, axis=1, keepdims=True) + 1e-06)


def norm_back(grad_normed, source, inverse, gain):
    grad_gain = jnp.sum(grad_normed * source * inverse, axis=0)
    scaled = grad_normed * gain
    grad_source = inverse * (
        scaled - source * inverse * inverse * jnp.mean(scaled * source, axis=1, keepdims=True)
    )
    return (grad_source, grad_gain)


def plain_shards(
    inputs, segments, valid_count, teacher, cotangent, w_proj, w_decay, b_decay, w_out,
    gain_ret, gain_ffn, w_gu, w_down,
):
    seq_count = lax.axis_size("seq")
    me_seq = lax.axis_index("seq")
    tokens = inputs[0]
    count, model_width = tokens.shape
    heads = w_decay.shape[1]
    head_dim = model_width // heads
    width = heads // seq_count
    rows = w_proj.shape[0]

    def mine(value, axis):
        return lax.dynamic_index_in_dim(value, me_seq, axis, keepdims=False)

    def spread(value, axis):
        wide = jnp.expand_dims(value, axis)
        return jnp.concatenate(
            [jnp.where(me_seq == s, wide, jnp.zeros_like(wide)) for s in range(seq_count)], axis
        )

    def gather(block):
        return lax.all_gather(block, "dp", axis=0, tiled=True)

    def gather_tokens(value):
        return lax.all_gather(value, "seq", axis=0, tiled=True)

    def sum_tokens(value):
        return lax.psum_scatter(
            value.astype(LOW), "seq", scatter_dimension=0, tiled=True
        ).astype(WIDE)

    def scatter(grad):
        return lax.psum_scatter(grad.astype(LOW), "dp", scatter_dimension=0, tiled=True)

    def sum_rows(grad):
        return lax.psum(scatter(grad), "seq").astype(WIDE)

    def sum_columns(grad, blocks):
        total = scatter(grad)
        pieces = lax.all_gather(total.reshape(total.shape[0], blocks, -1), "seq", axis=2)
        return pieces.reshape(total.shape[0], -1).astype(WIDE)

    decay = jnp.pad(w_decay, ((0, 0), (0, EXTRA - heads)))
    proj = mine(w_proj.reshape(rows, 4 * width, seq_count, -1), 2).reshape(rows, -1)
    proj_w = jnp.concatenate([gather(proj), gather(decay)], axis=1)
    out_w = mine(gather(w_out).reshape(width, seq_count, -1, model_width), 1).reshape(-1, model_width)
    gu_w = gather(mine(w_gu.reshape(rows, 2, seq_count, -1), 2).reshape(rows, -1))
    down_w = mine(gather(w_down).reshape(seq_count, -1, model_width), 0)
    units = down_w.shape[0]

    scale_one = rms(tokens)
    normed = gather_tokens((tokens * scale_one * gain_ret).astype(LOW))
    seg_col = gather_tokens(segments[0])[:, None]
    projected = dot(normed, proj_w)
    bias = jnp.pad(b_decay, (0, EXTRA - heads))[None]
    gated, kept, cum, cum_rows = retention(projected, bias, seg_col, seg_col.T, width, head_dim)
    mixed = tokens + sum_tokens(dot(gated, out_w))
    scale_two = rms(mixed)
    normed_ffn = gather_tokens((mixed * scale_two * gain_ffn).astype(LOW))
    gate_up = dot(normed_ffn, gu_w)
    gate_part, up_part = gate_up[:, :units], gate_up[:, units:]
    sigma = jax.nn.sigmoid(gate_part)
    activated = (gate_part * sigma * up_part).astype(LOW)
    result = mixed + sum_tokens(dot(activated, down_w))

    position = me_seq * count + jnp.arange(count, dtype=jnp.int32)
    valid_mask = (position < valid_count[0]).astype(WIDE)[:, None]
    mismatch = result - teacher[0]
    grad_out = cotangent[0] + valid_mask * mismatch
    squared_local = jnp.sum(valid_mask * mismatch * mismatch)
    count_local = jnp.sum(valid_mask)

    grad_ffn = gather_tokens(grad_out.astype(LOW))
    grad = dot(activated, grad_ffn, 0, 0)
    down_grad = sum_rows(spread(grad, 0).reshape(-1, model_width))
    grad_act = dot(grad_ffn, down_w, 1, 1)
    grad_gate = grad_act * up_part * sigma * (1.0 + gate_part * (1.0 - sigma))
    grad_up = grad_act * gate_part * sigma
    grad_both = jnp.concatenate([grad_gate, grad_up], axis=1).astype(LOW)
    gu_grad = sum_columns(dot(normed_ffn, grad_both, 0, 0), 2)
    grad_normed = sum_tokens(dot(grad_both, gu_w, 1, 1))
    grad_mid, gain_ffn_grad = norm_back(grad_normed, mixed, scale_two, gain_ffn)
    grad_mixed = grad_out + grad_mid
    grad_att = gather_tokens(grad_mixed.astype(LOW))
    grad = dot(gated, grad_att, 0, 0)
    out_grad = sum_rows(spread(grad.reshape(width, -1, model_width), 1).reshape(-1, model_width))
    grad_gated = dot(grad_att, out_w, 1, 1)
    grad_proj, bias_local = retention_back(
        projected, bias, kept, grad_gated, cum, cum_rows, seg_col, seg_col.T, width, head_dim
    )
    share = 4 * width * head_dim
    grad = dot(normed, grad_proj, 0, 0)
    proj_grad = sum_columns(grad[:, :share], 4 * width)
    decay_grad = sum_rows(grad[:, share : share + heads])
    grad_normed_one = sum_tokens(dot(grad_proj, proj_w, 1, 1))
    grad_first, gain_ret_grad = norm_back(grad_normed_one, tokens, scale_one, gain_ret)
    totals = lax.psum(
        (gain_ret_grad, gain_ffn_grad, bias_local[0], squared_local, count_local), ("dp", "seq")
    )
    return (
        result[None],
        (grad_mixed + grad_first)[None],
        proj_grad,
        decay_grad,
        totals[2][:heads],
        out_grad,
        totals[0],
        totals[1],
        gu_grad,
        down_grad,
        totals[3] / (totals[4] * model_width),
    )


def solution(mesh):
    rows = P("dp", None)
    in_specs = (
        P("dp", "seq", None),
        P("dp", "seq"),
        P("dp"),
        P("dp", "seq", None),
        P("dp", "seq", None),
        rows,
        rows,
        P(),
        rows,
        P(),
        P(),
        rows,
        rows,
    )
    out_specs = (
        P("dp", "seq", None),
        P("dp", "seq", None),
        rows,
        rows,
        P(),
        rows,
        P(),
        P(),
        rows,
        rows,
        P(),
    )
    sizes = dict(mesh.shape)
    shards = placed_shards if sizes["dp"] == 8 and sizes["seq"] == 4 else plain_shards
    return jax.shard_map(shards, mesh=mesh, in_specs=in_specs, out_specs=out_specs, check_vma=False)
```
